128 devices in a mesh: dom: 8 (over z, core), slab: 16 (over x, y).
Axes of the slice: x: 4, y: 4, z: 4, core: 2. Of those that a mesh axis runs over, the one named last changes fastest.
Arguments:
- nodes: bfloat16 [8, 16, 512, 128], P('dom', 'slab'), may hold values from -6 to 6
- edges: bfloat16 [8, 16, 8192, 128], P('dom', 'slab'), may hold values from -6 to 6
- coarse: bfloat16 [8, 16, 128, 128], P('dom', 'slab'), may hold values from -6 to 6
- senders: int32 [8, 16, 8192], P('dom', 'slab'), may hold values from 0 to 767
- receivers: int32 [8, 16, 8192], P('dom', 'slab'), may hold values from 0 to 511
- mirror_rows: int32 [8, 16, 4, 64], P('dom', 'slab'), may hold values from 0 to 511
- owner_device: int32 [8, 16, 512, 1], P('dom', 'slab'), may hold values from 0 to 127; in each aligned block of 512 rows (0 to 511, 512 to 1023, ..., all dimensions but the last counted through in order) at most 8 rows name the same one
- owner_slot: int32 [8, 16, 512], P('dom', 'slab'), may hold values from 0 to 127
- edge_first: bfloat16 [384, 128], replicated, may hold values from -0.3125 to 0.3125
- edge_bias: float32 [128], replicated, may hold values from -3 to 3
- edge_second: bfloat16 [128, 128], replicated, may hold values from -0.5 to 0.5
- edge_gain: float32 [128], replicated, may hold values from 0.1 to 1.9
- node_first: bfloat16 [256, 128], replicated, may hold values from -0.375 to 0.375
- node_bias: float32 [128], replicated, may hold values from -3 to 3
- node_second: bfloat16 [128, 128], replicated, may hold values from -0.5 to 0.5
- node_gain: float32 [128], replicated, may hold values from 0.1 to 1.9
- coarse_first: bfloat16 [256, 128], replicated, may hold values from -0.375 to 0.375
- coarse_bias: float32 [128], replicated, may hold values from -3 to 3
- coarse_second: bfloat16 [128, 128], replicated, may hold values from -0.5 to 0.5
- coarse_gain: float32 [128], replicated, may hold values from 0.1 to 1.9
- cot_nodes: bfloat16 [8, 16, 512, 128], P('dom', 'slab'), may hold values from -6 to 6
- cot_edges: bfloat16 [8, 16, 8192, 128], P('dom', 'slab'), may hold values from -6 to 6
- cot_coarse: bfloat16 [8, 16, 128, 128], P('dom', 'slab'), may hold values from -18 to 18
Outputs:
- new_nodes: bfloat16 [8, 16, 512, 128], P('dom', 'slab')
- new_edges: bfloat16 [8, 16, 8192, 128], P('dom', 'slab')
- new_coarse: bfloat16 [8, 16, 128, 128], P('dom', 'slab')
- grad_nodes: float32 [8, 16, 512, 128], P('dom', 'slab')
- grad_edges: float32 [8, 16, 8192, 128], P('dom', 'slab')
- grad_coarse: float32 [8, 16, 128, 128], P('dom', 'slab')
The draws below stay inside these ranges and needn't reach their ends.
Inputs may be any that keep to these rules, and one draw needn't show every extreme that they name: `owner_device`: among the rows of one partition no owner group is named more than 8 times, and some partition names one group exactly 8 times.
All inputs are finite; a program needn't handle non-finite values.
Results may differ from the reference program's by a relative error of at most 0.035.
Values may be sent and summed in bfloat16 or wider, within the bound.
A program may use at most 128 MiB of HBM per device.

```python
import math
import jax
import jax.numpy as jnp
import numpy as np
from jax import lax

L = 128
NODE_DEV = 512
EDGE_DEV = 8192
MIRROR = 64
COARSE_DEV = 128
CAP = 8
N_DOM = 8
N_SLAB = 16
DEVICES = 128


def set_ends(result, rng, low, top_value):
    shape = result.shape
    place = [jax.random.randint(jax.random.fold_in(rng, axis), (), 0, shape[axis]) for axis in range(len(shape))]
    result = result.at[tuple(place)].set(low)
    longest = shape.index(max(shape))
    place[longest] = (place[longest] + 1) % shape[longest]
    return result.at[tuple(place)].set(top_value)


def shard_levels(stream_key, shape, pieces, least, top_value):
    loudness = 1.0
    for position, shards_of in pieces:
        draws = jax.random.uniform(jax.random.fold_in(jax.random.fold_in(stream_key, 6), position), (shards_of,), jnp.float32, least / len(pieces), top_value / len(pieces))
        loudness = loudness * jnp.repeat(jnp.exp(draws), shape[position] // shards_of).reshape((-1,) + (1,) * (len(shape) - 1 - position))
    return loudness


def deal_out(own_key, own, number, rows, number_of, top, most, lean):
    ranking = jax.random.permutation(own_key, number_of)
    crowded, common = portions_of(number_of, rows * top, most, lean, True), portions_of(number_of, rows * top, most, lean, False)
    places = jnp.arange(number_of)

    def named(sizes, turn):
        used = int((sizes > 0).sum())
        fixed = max(1, used // 4)
        moved = fixed + (places - fixed + turn * (used - fixed)) % max(1, number_of - fixed)
        return jnp.zeros((number_of,), jnp.int32).at[ranking[jnp.where(places < fixed, places, moved)]].set(jnp.asarray(sizes, jnp.int32))

    sizes = jnp.where(number % 4 == 0, named(crowded, number // 4), named(common, number - number // 4 - 1))
    mixed = jax.random.permutation(jax.random.fold_in(own, 3), number_of)
    donor, receiver = mixed[0:number_of // 2 * 2:2], mixed[1:number_of // 2 * 2:2]
    margin = jnp.minimum(sizes[donor] - 1, most - sizes[receiver]) // 2
    margin = jnp.where((donor == ranking[0]) | (receiver == ranking[0]) | (sizes[receiver] == 0), 0, jnp.maximum(margin, 0))
    moved = jax.random.randint(jax.random.fold_in(own, 4), (number_of // 2,), 0, 1 << 20) % (margin + 1)
    sizes = sizes.at[donor].add(-moved).at[receiver].add(moved)
    items = jnp.searchsorted(jnp.cumsum(sizes), jnp.arange(rows * top), side="right").astype(jnp.int32)
    grid = items.reshape(top, rows).T
    grid = grid[jax.random.permutation(jax.random.fold_in(own, 1), rows)]
    turn = jax.random.randint(jax.random.fold_in(own, 2), (rows, 1), 0, top)
    return jnp.take_along_axis(grid, (jnp.arange(top)[None, :] + turn) % top, axis=1)


def portions_of(number_of, total, bound, skew, full):
    portions = [(1 << 20) // math.isqrt(grade ** skew) + 1 for grade in range(1, number_of + 1)]
    largest = bound if full else min(bound, max(-(-total // number_of), total * portions[0] // sum(portions)))
    least = 1 if total - largest >= number_of - 1 else 0
    counts, surplus = [largest] + [least] * (number_of - 1), total - largest - least * (number_of - 1)
    while surplus > 0:
        candidates = [i for i in range(1, number_of) if counts[i] < largest] or [i for i in range(1, number_of) if counts[i] < bound]
        pool, budget = sum([portions[i] for i in candidates]), surplus
        for i in candidates:
            more = min(bound - counts[i], max(1, budget * portions[i] // pool), surplus)
            counts[i] = counts[i] + more
            surplus = surplus - more
    return np.array(counts)


def scatter_about(own_key, extent, deviation, reach, split=(), held_as=jnp.bfloat16):
    factor_of = shard_levels(own_key, extent, split, -0.22, 0.18) if split else 1.0
    drawn = jax.random.normal(own_key, extent, jnp.float32) * deviation * factor_of
    return jnp.minimum(jnp.maximum(drawn, -reach), reach).astype(held_as)


def setup_inputs(seed: int = 0) -> dict:
    arg_keys = jax.random.split(jax.random.key(seed), 24)
    nodes = scatter_about(arg_keys[0], (N_DOM, N_SLAB, NODE_DEV, L), 1.0, 6.0, ((0, 8), (1, 16)))
    edges = scatter_about(arg_keys[1], (N_DOM, N_SLAB, EDGE_DEV, L), 1.0, 6.0, ((0, 8), (1, 16)))
    coarse = scatter_about(arg_keys[2], (N_DOM, N_SLAB, COARSE_DEV, L), 1.0, 6.0, ((0, 8), (1, 16)))
    senders = set_ends(jax.random.randint(arg_keys[3], (N_DOM, N_SLAB, EDGE_DEV), 0, NODE_DEV + 4 * MIRROR), jax.random.fold_in(arg_keys[3], 1), 0, (NODE_DEV + 4 * MIRROR) - 1).astype(jnp.int32)
    receivers = set_ends(jax.random.randint(arg_keys[4], (N_DOM, N_SLAB, EDGE_DEV), 0, NODE_DEV), jax.random.fold_in(arg_keys[4], 1), 0, NODE_DEV - 1).astype(jnp.int32)
    mirror_rows = set_ends(jax.random.randint(arg_keys[5], (N_DOM, N_SLAB, 4, MIRROR), 0, NODE_DEV), jax.random.fold_in(arg_keys[5], 1), 0, NODE_DEV - 1).astype(jnp.int32)
    owner_device_keys = jax.random.split(jax.random.fold_in(arg_keys[6], 1), N_DOM * N_SLAB * NODE_DEV // NODE_DEV)
    owner_device_turns = jax.random.permutation(jax.random.fold_in(arg_keys[6], 3), N_DOM * N_SLAB * NODE_DEV // NODE_DEV)
    owner_device = jax.vmap(lambda own, number: deal_out(jax.random.fold_in(arg_keys[6], 2), own, number, NODE_DEV, DEVICES, 1, CAP, 2))(owner_device_keys, owner_device_turns).reshape((N_DOM, N_SLAB, NODE_DEV, 1))
    owner_slot = set_ends(jax.random.randint(arg_keys[7], (N_DOM, N_SLAB, NODE_DEV), 0, COARSE_DEV), jax.random.fold_in(arg_keys[7], 1), 0, COARSE_DEV - 1).astype(jnp.int32)
    edge_first = scatter_about(arg_keys[8], (3 * L, L), (3 * L) ** -0.5, 0.3125)
    edge_bias = scatter_about(arg_keys[9], (L,), 0.5, 3.0, (), jnp.float32)
    edge_second = scatter_about(arg_keys[10], (L, L), L ** -0.5, 0.5)
    edge_gain = jnp.clip(1.0 + 0.18 * jax.random.normal(arg_keys[11], (L,), jnp.float32), 0.1, 1.9)
    node_first = scatter_about(arg_keys[12], (2 * L, L), (2 * L) ** -0.5, 0.375)
    node_bias = scatter_about(arg_keys[13], (L,), 0.5, 3.0, (), jnp.float32)
    node_second = scatter_about(arg_keys[14], (L, L), L ** -0.5, 0.5)
    node_gain = jnp.clip(1.0 + 0.18 * jax.random.normal(arg_keys[15], (L,), jnp.float32), 0.1, 1.9)
    coarse_first = scatter_about(arg_keys[16], (2 * L, L), (2 * L) ** -0.5, 0.375)
    coarse_bias = scatter_about(arg_keys[17], (L,), 0.5, 3.0, (), jnp.float32)
    coarse_second = scatter_about(arg_keys[18], (L, L), L ** -0.5, 0.5)
    coarse_gain = jnp.clip(1.0 + 0.18 * jax.random.normal(arg_keys[19], (L,), jnp.float32), 0.1, 1.9)
    cot_nodes = scatter_about(arg_keys[20], (N_DOM, N_SLAB, NODE_DEV, L), 1.0, 6.0, ((0, 8), (1, 16)))
    cot_edges = scatter_about(arg_keys[21], (N_DOM, N_SLAB, EDGE_DEV, L), 1.0, 6.0, ((0, 8), (1, 16)))
    cot_coarse = scatter_about(arg_keys[22], (N_DOM, N_SLAB, COARSE_DEV, L), 3.0, 18.0, ((0, 8), (1, 16)))
    return {"nodes": nodes, "edges": edges, "coarse": coarse, "senders": senders, "receivers": receivers, "mirror_rows": mirror_rows, "owner_device": owner_device, "owner_slot": owner_slot, "edge_first": edge_first, "edge_bias": edge_bias, "edge_second": edge_second, "edge_gain": edge_gain, "node_first": node_first, "node_bias": node_bias, "node_second": node_second, "node_gain": node_gain, "coarse_first": coarse_first, "coarse_bias": coarse_bias, "coarse_second": coarse_second, "coarse_gain": coarse_gain, "cot_nodes": cot_nodes, "cot_edges": cot_edges, "cot_coarse": cot_coarse}


eps = 1e-05

def mlp(inputs, first_weight, first_bias, second_weight, norm_gain):
    hidden = jnp.maximum(jnp.dot(inputs, first_weight, preferred_element_type=jnp.float32) + first_bias, 0.0).astype(jnp.bfloat16)
    mixed_out = jnp.dot(hidden, second_weight, preferred_element_type=jnp.float32)
    center = mixed_out - lax.optimization_barrier(jnp.mean(mixed_out, -1, keepdims=True))
    spread = lax.optimization_barrier(jnp.mean(center * center, -1, keepdims=True))
    return center * lax.rsqrt(spread + eps) * norm_gain

def fine_part(fine_rows, edge_rows, incoming, sender_ids, receiver_ids, edge_params, node_params):
    extended = jnp.concatenate([fine_rows, incoming], 0)
    source_rows = jnp.take(extended, sender_ids, axis=0)
    target_rows = jnp.take(fine_rows, receiver_ids, axis=0)
    edge_in = jnp.concatenate([edge_rows, source_rows, target_rows], -1).astype(jnp.bfloat16)
    update = mlp(edge_in, *edge_params)
    new_edges = (edge_rows + update).astype(jnp.bfloat16)
    summed = jax.ops.segment_sum(update, receiver_ids, num_segments=fine_rows.shape[0])
    node_in = jnp.concatenate([fine_rows, summed], -1).astype(jnp.bfloat16)
    middle = (fine_rows + mlp(node_in, *node_params)).astype(jnp.bfloat16)
    return (new_edges, middle)

def coarse_part(coarse_rows, pooled, coarse_params):
    coarse_in = jnp.concatenate([coarse_rows, pooled], -1).astype(jnp.bfloat16)
    return (coarse_rows + mlp(coarse_in, *coarse_params)).astype(jnp.bfloat16)

def reference(nodes, edges, coarse, senders, receivers, mirror_rows, owner_device, owner_slot, edge_first, edge_bias, edge_second, edge_gain, node_first, node_bias, node_second, node_gain, coarse_first, coarse_bias, coarse_second, coarse_gain, cot_nodes, cot_edges, cot_coarse):
    devices = N_DOM * N_SLAB
    feat_width = nodes.shape[-1]
    edge_params = (edge_first, edge_bias, edge_second, edge_gain)
    node_params = (node_first, node_bias, node_second, node_gain)
    coarse_params = (coarse_first, coarse_bias, coarse_second, coarse_gain)
    owners = (owner_device[..., 0] * COARSE_DEV + owner_slot).reshape(-1).astype(jnp.int32)

    def one_part(members):
        fine_rows, edge_rows, incoming, sender_ids, receiver_ids = members
        return fine_part(fine_rows, edge_rows, incoming, sender_ids, receiver_ids, edge_params, node_params)

    def forward(fine_nodes, edge_lats, top_rows):
        chosen = mirror_rows.reshape(N_DOM, N_SLAB, 4 * MIRROR, 1)
        outgoing = jnp.take_along_axis(fine_nodes, chosen, axis=2).reshape(N_DOM, N_SLAB, 4, MIRROR, feat_width)
        zero_dom = jnp.zeros((1, N_SLAB, MIRROR, feat_width), jnp.float32)
        zero_slab = jnp.zeros((N_DOM, 1, MIRROR, feat_width), jnp.float32)
        from_below = jnp.concatenate([zero_dom, outgoing[:-1, :, 0]], 0)
        from_above = jnp.concatenate([outgoing[1:, :, 1], zero_dom], 0)
        from_left = jnp.concatenate([zero_slab, outgoing[:, :-1, 2]], 1)
        from_right = jnp.concatenate([outgoing[:, 1:, 3], zero_slab], 1)
        incoming = jnp.stack([from_below, from_above, from_left, from_right], 2).reshape(devices, 4 * MIRROR, feat_width)
        new_edges, middle = lax.map(jax.checkpoint(one_part), (fine_nodes.reshape(devices, NODE_DEV, feat_width), edge_lats.reshape(devices, EDGE_DEV, feat_width), incoming, senders.reshape(devices, EDGE_DEV), receivers.reshape(devices, EDGE_DEV)))
        middle_wide = middle.astype(jnp.float32).reshape(devices * NODE_DEV, feat_width)
        pooled = jax.ops.segment_sum(middle_wide, owners, num_segments=devices * COARSE_DEV)
        new_top = coarse_part(top_rows.reshape(devices * COARSE_DEV, feat_width), pooled, coarse_params)
        new_fine = (middle_wide + jnp.take(new_top.astype(jnp.float32), owners, axis=0)).astype(jnp.bfloat16)
        return (new_fine.reshape(fine_nodes.shape), new_edges.reshape(edge_lats.shape), new_top.reshape(top_rows.shape))
    results, pullback = jax.vjp(forward, nodes.astype(jnp.float32), edges.astype(jnp.float32), coarse.astype(jnp.float32))
    gradients = pullback((cot_nodes, cot_edges, cot_coarse))
    return (results[0], results[1], results[2], gradients[0], gradients[1], gradients[2])
```

```python
import math

import jax
import jax.numpy as jnp
from jax import lax
from jax.experimental import pallas as pl
from jax.experimental.pallas import tpu as pltpu
from jax.sharding import PartitionSpec as P

BF = jnp.bfloat16
F32 = jnp.float32
CHUNK = 512

eps = 1e-05


def from_behind(value, axis, steps):
    count = lax.axis_size(axis)
    leading, last = (max(0, -steps), min(count, count - steps))
    return lax.ppermute(value, axis, [(source, source + steps) for source in range(leading, last)])


def mlp(inputs, first_weight, first_bias, second_weight, norm_gain):
    hidden = jnp.maximum(
        jnp.dot(inputs, first_weight, preferred_element_type=jnp.float32) + first_bias, 0.0
    ).astype(jnp.bfloat16)
    mixed_out = jnp.dot(hidden, second_weight, preferred_element_type=jnp.float32)
    center = mixed_out - jnp.mean(mixed_out, -1, keepdims=True)
    spread = jnp.mean(center * center, -1, keepdims=True)
    return center * lax.rsqrt(spread + eps) * norm_gain


def split_parts(values):
    high_part = lax.optimization_barrier(values.astype(jnp.bfloat16))
    remainder = values - high_part.astype(jnp.float32)
    middle_part = lax.optimization_barrier(remainder.astype(jnp.bfloat16))
    low_part = (remainder - middle_part.astype(jnp.float32)).astype(jnp.bfloat16)
    return jnp.concatenate([high_part, middle_part, low_part], -1)


def join_parts(totals, feat_width):
    return (
        totals[:, :feat_width]
        + totals[:, feat_width : 2 * feat_width]
        + totals[:, 2 * feat_width :]
    )


def select_matrix(indices, count):
    return (indices[:, None] == jnp.arange(count, dtype=jnp.int32)[None, :]).astype(jnp.bfloat16)


def pick_rows(indices, lookup_table):
    feat_width = lookup_table.shape[-1]
    is_exact = lookup_table.dtype == jnp.bfloat16
    operand = lookup_table if is_exact else split_parts(lookup_table)
    row_count = indices.shape[0]
    block_rows = math.gcd(row_count, 2048)
    id_blocks = indices.reshape(row_count // block_rows, block_rows)

    def one_block(id_block):
        return jnp.dot(
            select_matrix(id_block, lookup_table.shape[0]),
            operand,
            preferred_element_type=jnp.float32,
        )

    picked = lax.map(one_block, id_blocks).reshape(row_count, operand.shape[-1])
    return picked if is_exact else join_parts(picked, feat_width)


def add_rows(indices, values, count):
    feat_width = values.shape[-1]
    is_exact = values.dtype == jnp.bfloat16
    operand = values if is_exact else split_parts(values)
    row_count = indices.shape[0]
    block_rows = math.gcd(row_count, 2048)
    id_blocks = indices.reshape(row_count // block_rows, block_rows)
    value_blocks = operand.reshape(row_count // block_rows, block_rows, operand.shape[-1])

    def accumulate(running, members):
        id_block, value_block = members
        selector = select_matrix(id_block, count)
        return (
            running
            + lax.dot_general(
                selector, value_block, (((0,), (0,)), ((), ())), preferred_element_type=jnp.float32
            ),
            None,
        )

    running, unused = lax.scan(
        accumulate, jnp.zeros((count, operand.shape[-1]), jnp.float32), (id_blocks, value_blocks)
    )
    return running if is_exact else join_parts(running, feat_width)


def mm(a, b):
    return lax.dot_general(a, b, (((1,), (0,)), ((), ())), preferred_element_type=F32)


def mm_nt(a, b):
    return lax.dot_general(a, b, (((1,), (1,)), ((), ())), preferred_element_type=F32)


def centered(second):
    wide = second.astype(F32)
    return (wide - jnp.mean(wide, 1, keepdims=True)).astype(BF)


def averager():
    return jnp.full((128, 128), 1.0 / 128, BF)


def id_code(row):
    n = row.shape[1]
    low = jnp.broadcast_to((row & 127).astype(F32).astype(BF), (128, n))
    high = jnp.broadcast_to((row >> 7).astype(F32).astype(BF), (128, n))
    place = lax.broadcasted_iota(jnp.int32, (128, n), 0).astype(F32).astype(BF)
    return jnp.where(low == place, high, BF(-1))


def one_hots(code, blocks, axis):
    return jnp.concatenate([jnp.where(code == BF(k), BF(1), BF(0)) for k in range(blocks)], axis)


def halves(x):
    high = x.astype(BF)
    return jnp.concatenate([high, (x - high.astype(F32)).astype(BF)], 1)


def edge_forward(snd, rcv, lat, table, w_lat, second, gain, norm_o, hid_o, rstd_o, code_o, sum_o):
    sum_o[...] = jnp.zeros_like(sum_o)

    def body(i, carry):
        sl = pl.ds(pl.multiple_of(i * CHUNK, CHUNK), CHUNK)
        s_code, r_code = id_code(snd[:, sl]), id_code(rcv[:, sl])
        s_rows, r_rows = s_code.T, r_code.T
        code_o[sl, :] = r_rows
        x = jnp.concatenate([one_hots(s_rows, 6, 1), one_hots(r_rows, 4, 1), lat[sl, :]], 1)
        pre = mm(x, jnp.concatenate([table[...], w_lat], 0))
        hid = jnp.maximum(pre, 0.0).astype(BF)
        hid_o[sl, :] = hid
        center = mm(hid, second)
        rstd = lax.rsqrt(mm((center * center).astype(BF), averager()) + eps)
        norm = center * rstd
        norm_o[sl, :] = norm.astype(BF)
        rstd_o[sl, :] = rstd.astype(BF)
        sum_o[...] += mm(one_hots(r_code, 4, 0), halves(norm * gain))
        return carry

    lax.fori_loop(0, lat.shape[0] // CHUNK, body, 0)


def edge_backward(
    snd, rcv, code_i, cot_table, cot, lat, norm_i, hid_i, rstd_i, w_lat, second, gain, new_o, grad_o, table_o
):
    table_o[...] = jnp.zeros_like(table_o)

    def body(i, carry):
        sl = pl.ds(pl.multiple_of(i * CHUNK, CHUNK), CHUNK)
        cot_new = cot[sl, :].astype(F32)
        norm = norm_i[sl, :].astype(F32)
        new_o[sl, :] = (lat[sl, :].astype(F32) + norm * gain).astype(BF)
        scaled = (cot_new + mm(one_hots(code_i[sl, :], 4, 1), cot_table)) * gain
        along = mm((scaled * norm).astype(BF), averager())
        cot_mixed = (rstd_i[sl, :].astype(F32) * (scaled - norm * along)).astype(BF)
        cot_hid = mm_nt(cot_mixed, second)
        cot_pre = jnp.where(hid_i[sl, :].astype(F32) > 0, cot_hid, 0.0).astype(BF)
        grad_o[sl, :] = cot_new + mm_nt(cot_pre, w_lat)
        hots = jnp.concatenate(
            [one_hots(id_code(snd[:, sl]), 6, 0), one_hots(id_code(rcv[:, sl]), 4, 0)], 0
        )
        table_o[...] += mm(hots, cot_pre)
        return carry

    lax.fori_loop(0, lat.shape[0] // CHUNK, body, 0)


def forward_kernel(
    snd, rcv, lat, fine, arrived, e_first, e_bias, e_second, e_gain, n_first, n_bias, n_second, n_gain,
    norm_o, hid_o, rstd_o, code_o, middle_o, nhid_o, nnorm_o, nrstd_o, table, sums,
):
    table[:512, :] = mm(fine[...], e_first[128:256, :]).astype(BF)
    table[512:768, :] = mm(arrived[...], e_first[128:256, :]).astype(BF)
    table[768:, :] = (mm(fine[...], e_first[256:, :]) + e_bias[...]).astype(BF)
    edge_forward(
        snd, rcv, lat, table, e_first[:128, :], centered(e_second[...]), e_gain[...],
        norm_o, hid_o, rstd_o, code_o, sums,
    )
    summed = (sums[:, :128] + sums[:, 128:]).astype(BF)
    hid = jnp.maximum(mm(jnp.concatenate([fine[...], summed], 1), n_first[...]) + n_bias[...], 0.0)
    hid = hid.astype(BF)
    center = mm(hid, centered(n_second[...]))
    rstd = lax.rsqrt(jnp.mean(center * center, 1, keepdims=True) + eps)
    norm = center * rstd
    middle_o[...] = (fine[...].astype(F32) + norm * n_gain[...]).astype(BF)
    nhid_o[...] = hid
    nnorm_o[...] = norm
    nrstd_o[...] = jnp.broadcast_to(rstd, norm.shape)


def backward_kernel(
    snd, rcv, lat, cot, norm_i, hid_i, rstd_i, code_i, nhid, nnorm, nrstd, cot_mid,
    e_first, e_second, e_gain, n_first, n_second, n_gain,
    new_o, grad_o, fine_o, mirror_o, table,
):
    up = cot_mid[...].astype(F32)
    scaled = up * n_gain[...]
    norm = nnorm[...]
    along = jnp.mean(scaled * norm, 1, keepdims=True)
    cot_mixed = (nrstd[...] * (scaled - norm * along)).astype(BF)
    cot_hid = mm_nt(cot_mixed, centered(n_second[...]))
    cot_pre = jnp.where(nhid[...].astype(F32) > 0, cot_hid, 0.0).astype(BF)
    both = mm_nt(cot_pre, n_first[...])
    edge_backward(
        snd, rcv, code_i, both[:, 128:].astype(BF), cot, lat, norm_i, hid_i, rstd_i,
        e_first[:128, :], centered(e_second[...]), e_gain[...], new_o, grad_o, table,
    )
    w_src, w_tgt = e_first[128:256, :], e_first[256:, :]
    fine_o[...] = (
        up + both[:, :128] + mm_nt(table[:512, :].astype(BF), w_src) + mm_nt(table[768:, :].astype(BF), w_tgt)
    )
    mirror_o[...] = mm_nt(table[512:768, :].astype(BF), w_src)


VM = pl.BlockSpec(memory_space=pltpu.VMEM)


def shaped(*sizes, dtype=BF):
    return jax.ShapeDtypeStruct(sizes, dtype)


def run_forward(*operands):
    return pl.pallas_call(
        forward_kernel,
        out_shape=[shaped(8192, 128)] * 4 + [shaped(512, 128)] * 2 + [shaped(512, 128, dtype=F32)] * 2,
        in_specs=[VM] * len(operands),
        out_specs=[VM] * 8,
        scratch_shapes=[pltpu.VMEM((1280, 128), BF), pltpu.VMEM((512, 256), F32)],
        compiler_params=pltpu.CompilerParams(vmem_limit_bytes=50 << 20),
        name="forward",
    )(*operands)


def run_backward(*operands):
    return pl.pallas_call(
        backward_kernel,
        out_shape=[
            shaped(8192, 128), shaped(8192, 128, dtype=F32), shaped(512, 128, dtype=F32), shaped(256, 128, dtype=F32)
        ],
        in_specs=[VM] * len(operands),
        out_specs=[VM] * 4,
        scratch_shapes=[pltpu.VMEM((1280, 128), F32)],
        compiler_params=pltpu.CompilerParams(vmem_limit_bytes=50 << 20),
        name="backward",
    )(*operands)


def coarse_part(coarse_rows, pooled, coarse_params):
    coarse_in = jnp.concatenate([coarse_rows, pooled], -1).astype(jnp.bfloat16)
    return (coarse_rows + mlp(coarse_in, *coarse_params)).astype(jnp.bfloat16)


def pool_send(send_rows, send_slots, dom_count, slab_count, capacity):
    feat_width = send_rows.shape[-1]
    got_rows, got_slots = (
        lax.all_to_all(
            send_rows.reshape(dom_count * slab_count, capacity, feat_width),
            ("dom", "slab"),
            split_axis=0,
            concat_axis=0,
            tiled=True,
        ),
        lax.all_to_all(
            send_slots.reshape(dom_count * slab_count, capacity),
            ("dom", "slab"),
            split_axis=0,
            concat_axis=0,
            tiled=True,
        ),
    )
    return (got_rows.reshape(-1, feat_width), got_slots.reshape(-1))


def reply_rows(row_block, dom_count, slab_count, capacity):
    feat_width = row_block.shape[-1]
    moved = lax.all_to_all(
        row_block.reshape(dom_count * slab_count, capacity, feat_width),
        ("dom", "slab"),
        split_axis=0,
        concat_axis=0,
        tiled=True,
    )
    return moved.reshape(-1, feat_width)


def send_cotangents(row_block, dom_count, slab_count, capacity):
    feat_width = row_block.shape[-1]
    moved = lax.all_to_all(
        row_block.reshape(dom_count * slab_count, capacity, feat_width),
        ("dom", "slab"),
        split_axis=0,
        concat_axis=0,
        tiled=True,
    )
    return moved.reshape(-1, feat_width)


def return_grads(row_block, dom_count, slab_count, capacity):
    feat_width = row_block.shape[-1]
    moved = lax.all_to_all(
        row_block.reshape(dom_count * slab_count, capacity, feat_width),
        ("dom", "slab"),
        split_axis=0,
        concat_axis=0,
        tiled=True,
    )
    return moved.reshape(-1, feat_width)


def local(
    nodes,
    edges,
    coarse,
    senders,
    receivers,
    mirror_rows,
    owner_device,
    owner_slot,
    edge_first,
    edge_bias,
    edge_second,
    edge_gain,
    node_first,
    node_bias,
    node_second,
    node_gain,
    coarse_first,
    coarse_bias,
    coarse_second,
    coarse_gain,
    cot_nodes,
    cot_edges,
    cot_coarse,
):
    coarse_params = (coarse_first, coarse_bias, coarse_second, coarse_gain)
    feat_width = nodes.shape[-1]
    node_count = nodes.shape[2]
    coarse_count = coarse.shape[2]
    dom_count = lax.axis_size("dom")
    slab_count = lax.axis_size("slab")
    devices = dom_count * slab_count
    capacity = 2 * node_count // devices
    slot_total = devices * capacity
    node_table = nodes[0, 0]
    coarse_rows = coarse[0, 0].astype(jnp.float32)
    sender_ids = senders[0, 0]
    receiver_ids = receivers[0, 0]
    chosen = mirror_rows[0, 0].reshape(-1)
    mirror_count = mirror_rows.shape[3]
    outgoing = (
        pick_rows(chosen, node_table).astype(jnp.bfloat16).reshape(4, mirror_count, feat_width)
    )
    arrivals = []
    for block_id, shift_by in ((0, 1), (1, -1)):
        arrivals.append(from_behind(outgoing[block_id], "dom", shift_by))
    for block_id, shift_by in ((2, 1), (3, -1)):
        arrivals.append(from_behind(outgoing[block_id], "slab", shift_by))
    gains = [v.reshape(1, feat_width) for v in (edge_bias, edge_gain, node_bias, node_gain)]
    snd, rcv = sender_ids.reshape(1, -1), receiver_ids.reshape(1, -1)
    norm, hid, rstd, code, middle, nhid, nnorm, nrstd = run_forward(
        snd, rcv, edges[0, 0], node_table, jnp.concatenate(arrivals, 0),
        edge_first, gains[0], edge_second, gains[1], node_first, gains[2], node_second, gains[3],
    )
    owner_dev = owner_device[0, 0, :, 0]
    owner_pos = owner_slot[0, 0]
    group_hot = select_matrix(owner_dev, devices)
    positions = jnp.arange(node_count, dtype=jnp.int32)
    lower_mask = (positions[:, None] > positions[None, :]).astype(jnp.bfloat16)
    before = jnp.dot(lower_mask, group_hot, preferred_element_type=jnp.float32)
    earlier = jnp.sum(before * group_hot.astype(jnp.float32), 1).astype(jnp.int32)
    send_index = owner_dev * capacity + earlier
    slot_columns = jnp.stack(
        [owner_pos.astype(jnp.float32), jnp.ones((node_count,), jnp.float32)], -1
    )
    slot_sums = add_rows(send_index, slot_columns, slot_total)
    send_slots = jnp.where(slot_sums[:, 1] > 0.5, slot_sums[:, 0], float(coarse_count)).astype(
        jnp.int32
    )
    cot_fine = cot_nodes[0, 0]

    def coarse_step(rows_in, pooled_in):
        return coarse_part(rows_in, pooled_in, coarse_params)

    send_rows = add_rows(send_index, middle, slot_total).astype(jnp.bfloat16)
    got_rows, flat_slots = pool_send(send_rows, send_slots, dom_count, slab_count, capacity)
    pooled = add_rows(flat_slots, got_rows, coarse_count)
    new_coarse, coarse_pullback = jax.vjp(coarse_step, coarse_rows, pooled)
    lookup = pick_rows(flat_slots, new_coarse)
    answered = reply_rows(lookup.astype(jnp.bfloat16), dom_count, slab_count, capacity)
    lifted = pick_rows(send_index, answered)
    to_owner = add_rows(send_index, cot_fine, slot_total).astype(jnp.bfloat16)
    at_owner = send_cotangents(to_owner, dom_count, slab_count, capacity)
    coarse_cot = add_rows(flat_slots, at_owner, coarse_count)
    cot_top = cot_coarse[0, 0] + coarse_cot.astype(jnp.bfloat16)
    grad_top, grad_pooled = coarse_pullback(cot_top)
    to_fine = pick_rows(flat_slots, grad_pooled)
    at_fine = return_grads(to_fine, dom_count, slab_count, capacity)
    from_owner = pick_rows(send_index, at_fine)
    new_nodes = (middle.astype(jnp.float32) + lifted).astype(jnp.bfloat16)
    cot_middle = (cot_fine.astype(jnp.float32) + from_owner).astype(jnp.bfloat16)
    new_edges, grad_lat, grad_fine, mirrored = run_backward(
        snd, rcv, edges[0, 0], cot_edges[0, 0], norm, hid, rstd, code, nhid, nnorm, nrstd, cot_middle,
        edge_first, edge_second, gains[1], node_first, node_second, gains[3],
    )
    pieces = mirrored.reshape(4, mirror_count, feat_width)
    returned = []
    for block_id, shift_by in ((0, -1), (1, 1)):
        returned.append(from_behind(pieces[block_id], "dom", shift_by))
    for block_id, shift_by in ((2, -1), (3, 1)):
        returned.append(from_behind(pieces[block_id], "slab", shift_by))
    grad_fine = grad_fine + add_rows(chosen, jnp.concatenate(returned, 0), node_count)
    return (
        new_nodes[None, None],
        new_edges[None, None],
        new_coarse[None, None],
        grad_fine[None, None],
        grad_lat[None, None],
        grad_top[None, None],
    )


def solution(mesh):
    in_specs = (
        P("dom", "slab", None, None),
        P("dom", "slab", None, None),
        P("dom", "slab", None, None),
        P("dom", "slab", None),
        P("dom", "slab", None),
        P("dom", "slab", None, None),
        P("dom", "slab", None, None),
        P("dom", "slab", None),
        P(),
        P(),
        P(),
        P(),
        P(),
        P(),
        P(),
        P(),
        P(),
        P(),
        P(),
        P(),
        P("dom", "slab", None, None),
        P("dom", "slab", None, None),
        P("dom", "slab", None, None),
    )
    out_specs = (
        P("dom", "slab", None, None),
        P("dom", "slab", None, None),
        P("dom", "slab", None, None),
        P("dom", "slab", None, None),
        P("dom", "slab", None, None),
        P("dom", "slab", None, None),
    )
    return jax.shard_map(local, mesh=mesh, in_specs=in_specs, out_specs=out_specs, check_vma=False)
```

```python
import functools

import jax
import jax.numpy as jnp
from jax import lax
from jax.experimental import pallas as pl
from jax.experimental.pallas import tpu as pltpu
from jax.sharding import PartitionSpec as P

eps = 1e-05
BF = jnp.bfloat16
F32 = jnp.float32
MESH = pl.DeviceIdType.MESH
DOM, SLAB, DEVICES = 8, 16, 128
NODES, EDGES, MIRROR, CAP, L = 512, 8192, 64, 8, 128
CHUNK = 2048
STEPS = EDGES // CHUNK


def mm(a, b):
    return lax.dot_general(a, b, (((1,), (0,)), ((), ())), preferred_element_type=F32)


def mm_nt(a, b):
    return lax.dot_general(a, b, (((1,), (1,)), ((), ())), preferred_element_type=F32)


def averager():
    return jnp.full((L, L), 1.0 / L, BF)


def id_code(row):
    n = row.shape[1]
    low = jnp.broadcast_to((row & 127).astype(F32).astype(BF), (128, n))
    high = jnp.broadcast_to((row >> 7).astype(F32).astype(BF), (128, n))
    place = lax.broadcasted_iota(jnp.int32, (128, n), 0).astype(F32).astype(BF)
    return jnp.where(low == place, high, BF(-1))


def one_hots(code, blocks, axis):
    return jnp.concatenate([jnp.where(code == BF(k), BF(1), BF(0)) for k in range(blocks)], axis)


def halves(x):
    high = x.astype(BF)
    return jnp.concatenate([high, (x - high.astype(F32)).astype(BF)], 1)


def normed(hid, second):
    mixed = mm(hid, second)
    center = mixed - jnp.mean(mixed, 1, keepdims=True)
    rstd = lax.rsqrt(jnp.mean(center * center, 1, keepdims=True) + eps)
    return center * rstd, rstd


def layer(rows, added, first, bias, second):
    pre = mm(jnp.concatenate([rows, added.astype(BF)], 1), first) + bias
    hid = jnp.maximum(pre, 0.0).astype(BF)
    norm, rstd = normed(hid, second)
    return hid, norm, rstd


def layer_back(cot, hid, norm, rstd, first, second, gain):
    scaled = cot * gain
    along = jnp.mean(scaled * norm, 1, keepdims=True)
    cot_mixed = rstd * (scaled - jnp.mean(scaled, 1, keepdims=True) - norm * along)
    cot_hid = mm_nt(cot_mixed.astype(BF), second)
    cot_pre = jnp.where(hid.astype(F32) > 0, cot_hid, 0.0).astype(BF)
    return mm_nt(cot_pre, first)


def edge_forward(snd, rcv, lat, table, mixer, gain, norm_o, hid_o, rstd_o, code_o, sums, write):
    sums[...] = jnp.zeros_like(sums)

    def body(i, carry):
        sl = pl.ds(pl.multiple_of(i * CHUNK, CHUNK), CHUNK)
        s_code, r_code = id_code(snd[:, sl]), id_code(rcv[:, sl])
        s_rows, r_rows = s_code.T, r_code.T
        code_o[sl, :] = r_rows
        rows = lat[sl, :]
        pre = mm(jnp.concatenate([one_hots(s_rows, 6, 1), one_hots(r_rows, 4, 1), rows], 1), table[...])
        hid = jnp.maximum(pre[:, :L] + pre[:, L:], 0.0).astype(BF)
        hid_o[sl, :] = hid
        mixed = mm(hid, mixer)
        center = mixed[:, :L] - mixed[:, L:]
        rstd = lax.rsqrt(mm((center * center).astype(BF), averager()) + eps)
        norm = center * rstd
        norm_o[sl, :] = norm.astype(BF)
        rstd_o[sl, :] = rstd.astype(BF)
        update = norm * gain
        write(i, sl, (rows.astype(F32) + update).astype(BF))
        sums[...] += mm(one_hots(r_code, 4, 0), halves(update))
        return carry

    lax.fori_loop(0, STEPS, body, 0)


def edge_backward(snd, rcv, code_i, cot_table, cot, norm_i, hid_i, rstd_i, w_lat, second, gain, table_o, write):
    table_o[...] = jnp.zeros_like(table_o)

    def body(i, carry):
        sl = pl.ds(pl.multiple_of(i * CHUNK, CHUNK), CHUNK)
        cot_new = cot[sl, :].astype(F32)
        norm = norm_i[sl, :].astype(F32)
        scaled = (cot_new + mm(one_hots(code_i[sl, :], 4, 1), cot_table)) * gain
        along = mm((scaled * norm).astype(BF), averager())
        cot_mixed = (rstd_i[sl, :].astype(F32) * (scaled - norm * along)).astype(BF)
        cot_hid = mm_nt(cot_mixed, second)
        cot_pre = jnp.where(hid_i[sl, :].astype(F32) > 0, cot_hid, 0.0).astype(BF)
        write(i, sl, (cot_new + mm_nt(cot_pre, w_lat)).astype(BF))
        hots = jnp.concatenate([one_hots(id_code(snd[:, sl]), 6, 0), one_hots(id_code(rcv[:, sl]), 4, 0)], 0)
        table_o[...] += mm(hots, cot_pre)
        return carry

    lax.fori_loop(0, STEPS, body, 0)


def kernel(
    snd, rcv, chosen, own_dev, own_slot, lat_h, cot_h, fine, top, cot_fine, cot_top,
    e_first, e_bias, e_second, e_gain, n_first, n_bias, n_second, n_gain, c_first, c_bias, c_second, c_gain,
    new_nodes_o, new_edges_o, new_coarse_o, grad_nodes_o, grad_edges_o, grad_coarse_o,
    lat, cot, norm, hid, rstd, code, new_v, grad_v, table, sums, back_table, pick,
    mir_out, mir_in, early_out, early_in, mid_out, mid_in, grad_out, grad_in, row_out, row_in, ret_out, ret_in,
    load_sem, new_sem, grad_sem, mir_s, mir_r, ret_s, ret_r, early_s, early_r, mid_s, mid_r,
    gback_s, gback_r, row_s, row_r,
):
    dom, slab = lax.axis_index("dom"), lax.axis_index("slab")
    me = dom * SLAB + slab

    load_lat = pltpu.make_async_copy(lat_h, lat, load_sem.at[0])
    load_cot = pltpu.make_async_copy(cot_h, cot, load_sem.at[1])
    load_lat.start()
    load_cot.start()

    def peers(act):
        def body(step, carry):
            other = lax.rem(me + step, DEVICES)
            act(other, (other // SLAB, lax.rem(other, SLAB)))
            return carry

        lax.fori_loop(1, DEVICES, body, 0)

    barrier = pltpu.get_barrier_semaphore()
    peers(lambda other, place: pl.semaphore_signal(barrier, inc=1, device_id=place, device_id_type=MESH))

    def exchange(out, land, send, recv):
        def start(other, place):
            pltpu.make_async_remote_copy(
                src_ref=out.at[other], dst_ref=land.at[me], send_sem=send, recv_sem=recv,
                device_id=place, device_id_type=MESH,
            ).start()

        peers(start)
        land[me] = out[me]

    def finish(out, land, send, recv):
        for ref, sem in ((land, recv), (out, send)):
            whole = ref.at[pl.ds(0, DEVICES - 1)]
            pltpu.make_async_copy(whole, whole, sem).wait()

    def blocks(wide):
        return wide.reshape(DEVICES, CAP, L)

    def rows_of(land):
        return land[...].astype(F32).reshape(DEVICES * CAP, L).astype(BF)

    below, above = (dom - 1, slab), (dom + 1, slab)
    left, right = (dom, slab - 1), (dom, slab + 1)
    has = {"below": dom > 0, "above": dom < DOM - 1, "left": slab > 0, "right": slab < SLAB - 1}
    spot = {"below": below, "above": above, "left": left, "right": right}

    def mirrors(out, land, send, recv, targets, sources):
        copies = [
            pltpu.make_async_remote_copy(
                src_ref=out.at[k], dst_ref=land.at[k], send_sem=send.at[k], recv_sem=recv.at[k],
                device_id=spot[targets[k]], device_id_type=MESH,
            )
            for k in range(4)
        ]
        for k in range(4):
            pl.when(has[targets[k]])(copies[k].start)
            pl.when(jnp.logical_not(has[sources[k]]))(lambda k=k: land.__setitem__(k, jnp.zeros((MIRROR, L), BF)))

        def wait():
            for k in range(4):
                pl.when(has[sources[k]])(copies[k].wait_recv)
                pl.when(has[targets[k]])(copies[k].wait_send)

        return wait

    picked = jnp.concatenate([chosen[k : k + 1, :] for k in range(4)], 1)
    chosen_code = id_code(picked)
    mir_out[...] = mm(one_hots(chosen_code.T, 4, 1), fine[...]).astype(BF).reshape(4, MIRROR, L)

    owner = own_dev[...]
    group = one_hots(id_code(owner), 1, 0)
    place = lax.broadcasted_iota(jnp.int32, (NODES, NODES), 0)
    earlier = jnp.where(place < lax.broadcasted_iota(jnp.int32, (NODES, NODES), 1), 1.0, 0.0).astype(BF)
    rank = jnp.sum(mm(group, earlier) * group.astype(F32), 0, keepdims=True)
    send_code = id_code(owner * CAP + rank.astype(jnp.int32))
    pick[...] = one_hots(send_code, CAP, 0)
    slot_rows = jnp.broadcast_to((own_slot[...] + 1).astype(F32).astype(BF), (L, NODES)).T
    early = mm(pick[...], jnp.concatenate([cot_fine[...], slot_rows], 1))
    early_out[...] = jnp.concatenate([blocks(early[:, :L]), blocks(early[:, L:])], 1).astype(BF)

    pl.semaphore_wait(barrier, DEVICES - 1)
    mirror_wait = mirrors(
        mir_out, mir_in, mir_s, mir_r, ("above", "below", "right", "left"), ("below", "above", "left", "right")
    )
    exchange(early_out, early_in, early_s, early_r)

    w_lat, w_src, w_tgt = e_first[:L, :], e_first[L : 2 * L, :], e_first[2 * L :, :]
    table[:NODES, :] = halves(mm(fine[...], w_src))
    table[6 * L : 10 * L, :] = halves(mm(fine[...], w_tgt) + e_bias[...])
    table[10 * L :, :] = jnp.concatenate([w_lat, jnp.zeros((L, L), BF)], 1)
    second = e_second[...].astype(F32)
    second_mean = jnp.broadcast_to(jnp.mean(second, 1, keepdims=True), (L, L))
    mixer = jnp.concatenate([e_second[...], second_mean.astype(BF)], 1)
    mirror_wait()
    table[NODES : 6 * L, :] = halves(mm(mir_in[...].reshape(4 * MIRROR, L), w_src))
    load_lat.wait()

    def write_new(i, sl, value):
        new_v[sl, :] = value
        pltpu.make_async_copy(new_v.at[sl], new_edges_o.at[sl], new_sem.at[i]).start()

    edge_forward(snd, rcv, lat, table, mixer, e_gain[...], norm, hid, rstd, code, sums, write_new)

    summed = sums[:, :L] + sums[:, L:]
    n_hid, n_norm, n_rstd = layer(fine[...], summed, n_first[...], n_bias[...], n_second[...])
    middle = (fine[...].astype(F32) + n_norm * n_gain[...]).astype(BF)
    mid_out[...] = blocks(mm(pick[...], middle)).astype(BF)
    exchange(mid_out, mid_in, mid_s, mid_r)

    finish(early_out, early_in, early_s, early_r)
    early_rows = early_in[...].astype(F32)
    slots = early_rows[:, CAP:].reshape(DEVICES * CAP, L)
    lane = lax.broadcasted_iota(jnp.int32, (DEVICES * CAP, L), 1).astype(F32)
    held = jnp.where(slots == lane + 1.0, 1.0, 0.0).astype(BF)
    gather = held.T
    cot_at = mm(gather, early_rows[:, :CAP].reshape(DEVICES * CAP, L).astype(BF))
    cot_new = (cot_top[...].astype(F32) + cot_at.astype(BF).astype(F32)).astype(BF).astype(F32)
    finish(mid_out, mid_in, mid_s, mid_r)
    pooled = mm(gather, rows_of(mid_in))
    c_hid, c_norm, c_rstd = layer(top[...], pooled, c_first[...], c_bias[...], c_second[...])
    new_top = (top[...].astype(F32) + c_norm * c_gain[...]).astype(BF)
    c_back = layer_back(cot_new, c_hid, c_norm, c_rstd, c_first[...], c_second[...], c_gain[...])
    grad_out[...] = blocks(mm(held, c_back[:, L:].astype(BF))).astype(BF)
    exchange(grad_out, grad_in, gback_s, gback_r)
    row_out[...] = blocks(mm(held, new_top)).astype(BF)
    exchange(row_out, row_in, row_s, row_r)
    new_coarse_o[...] = new_top
    grad_coarse_o[...] = cot_new + c_back[:, :L]

    second_c = (second - second_mean).astype(BF)
    load_cot.wait()
    finish(grad_out, grad_in, gback_s, gback_r)
    reply = one_hots(send_code.T, CAP, 1)
    cot_mid = (cot_fine[...].astype(F32) + mm(reply, rows_of(grad_in))).astype(BF).astype(F32)
    n_back = layer_back(cot_mid, n_hid, n_norm, n_rstd, n_first[...], n_second[...], n_gain[...])

    def write_grad(i, sl, value):
        grad_v[sl, :] = value
        pltpu.make_async_copy(grad_v.at[sl], grad_edges_o.at[sl], grad_sem.at[i]).start()

    edge_backward(
        snd, rcv, code, n_back[:, L:].astype(BF), cot, norm, hid, rstd, w_lat, second_c, e_gain[...],
        back_table, write_grad,
    )
    back = mm_nt(back_table[NODES : 6 * L, :].astype(BF), w_src)
    ret_out[...] = back.astype(BF).reshape(4, MIRROR, L)
    return_wait = mirrors(
        ret_out, ret_in, ret_s, ret_r, ("below", "above", "left", "right"), ("above", "below", "right", "left")
    )
    total = cot_mid + n_back[:, :L] + mm_nt(back_table[:NODES, :].astype(BF), w_src)
    total = total + mm_nt(back_table[6 * L :, :].astype(BF), w_tgt)
    finish(row_out, row_in, row_s, row_r)
    new_nodes_o[...] = (middle.astype(F32) + mm(reply, rows_of(row_in))).astype(BF)
    return_wait()
    grad_nodes_o[...] = total + mm(one_hots(chosen_code, 4, 0), ret_in[...].reshape(4 * MIRROR, L))
    for i in range(STEPS):
        sl = pl.ds(i * CHUNK, CHUNK)
        pltpu.make_async_copy(new_v.at[sl], new_edges_o.at[sl], new_sem.at[i]).wait()
        pltpu.make_async_copy(grad_v.at[sl], grad_edges_o.at[sl], grad_sem.at[i]).wait()


VM = pl.BlockSpec(memory_space=pltpu.VMEM)
ANY = pl.BlockSpec(memory_space=pl.ANY)


def shaped(*sizes, dtype=BF):
    return jax.ShapeDtypeStruct(sizes, dtype)


def local(
    nodes, edges, coarse, senders, receivers, mirror_rows, owner_device, owner_slot,
    edge_first, edge_bias, edge_second, edge_gain, node_first, node_bias, node_second, node_gain,
    coarse_first, coarse_bias, coarse_second, coarse_gain, cot_nodes, cot_edges, cot_coarse,
):
    def line(v):
        return v.reshape(1, -1)

    edge_rows = [pltpu.VMEM((EDGES, L), BF)] * 8
    pair = lambda *sizes: [pltpu.VMEM(sizes, BF)] * 2
    dma = pltpu.SemaphoreType.DMA
    outs = pl.pallas_call(
        kernel,
        out_shape=[
            shaped(NODES, L), shaped(EDGES, L), shaped(128, L),
            shaped(NODES, L, dtype=F32), shaped(EDGES, L), shaped(128, L, dtype=F32),
        ],
        in_specs=[VM] * 5 + [ANY] * 2 + [VM] * 16,
        out_specs=[VM, ANY, VM, VM, ANY, VM],
        scratch_shapes=edge_rows
        + [
            pltpu.VMEM((11 * L, 2 * L), BF), pltpu.VMEM((NODES, 2 * L), F32), pltpu.VMEM((10 * L, L), F32),
            pltpu.VMEM((DEVICES * CAP, NODES), BF),
        ]
        + pair(4, MIRROR, L) + pair(DEVICES, 2 * CAP, L) + pair(DEVICES, CAP, L) * 3 + pair(4, MIRROR, L)
        + [dma((2,)), dma((STEPS,)), dma((STEPS,))] + [dma((4,))] * 4 + [dma] * 8,
        compiler_params=pltpu.CompilerParams(
            vmem_limit_bytes=58 << 20, collective_id=0, has_side_effects=True
        ),
        name="mesh_layer",
    )(
        line(senders), line(receivers), mirror_rows[0, 0], line(owner_device), line(owner_slot),
        edges[0, 0], cot_edges[0, 0], nodes[0, 0], coarse[0, 0], cot_nodes[0, 0], cot_coarse[0, 0],
        edge_first, line(edge_bias), edge_second, line(edge_gain),
        node_first, line(node_bias), node_second, line(node_gain),
        coarse_first, line(coarse_bias), coarse_second, line(coarse_gain),
    )
    outs = list(outs)
    outs[4] = outs[4].astype(F32)
    return tuple(o[None, None] for o in outs)


def solution(mesh):
    four, three, whole = P("dom", "slab", None, None), P("dom", "slab", None), P()
    in_specs = (four, four, four, three, three, four, four, three) + (whole,) * 12 + (four,) * 3
    return jax.shard_map(local, mesh=mesh, in_specs=in_specs, out_specs=(four,) * 6, check_vma=False)
```

```python
import functools

import jax
import jax.numpy as jnp
from jax import lax
from jax.experimental import pallas as pl
from jax.experimental.pallas import tpu as pltpu
from jax.sharding import PartitionSpec as P

eps = 1e-05
BF = jnp.bfloat16
F32 = jnp.float32
MESH = pl.DeviceIdType.MESH
DOM, SLAB, DEVICES = 8, 16, 128
NODES, EDGES, MIRROR, CAP, L = 512, 8192, 64, 8, 128
CHUNK = 2048
STEPS = EDGES // CHUNK
PARTS = 4
INPUTS = 23


def mm(a, b):
    return lax.dot_general(a, b, (((1,), (0,)), ((), ())), preferred_element_type=F32)


def mm_nt(a, b):
    return lax.dot_general(a, b, (((1,), (1,)), ((), ())), preferred_element_type=F32)


def averager():
    return jnp.full((L, L), 1.0 / L, BF)


def id_code(row):
    n = row.shape[1]
    low = jnp.broadcast_to((row & 127).astype(F32).astype(BF), (128, n))
    high = jnp.broadcast_to((row >> 7).astype(F32).astype(BF), (128, n))
    place = lax.broadcasted_iota(jnp.int32, (128, n), 0).astype(F32).astype(BF)
    return jnp.where(low == place, high, BF(-1))


def one_hots(code, blocks, axis):
    return jnp.concatenate([jnp.where(code == BF(k), BF(1), BF(0)) for k in range(blocks)], axis)


def halves(x):
    high = x.astype(BF)
    return jnp.concatenate([high, (x - high.astype(F32)).astype(BF)], 1)


def normed(hid, second):
    mixed = mm(hid, second)
    center = mixed - jnp.mean(mixed, 1, keepdims=True)
    rstd = lax.rsqrt(jnp.mean(center * center, 1, keepdims=True) + eps)
    return center * rstd, rstd


def layer(rows, added, first, bias, second):
    pre = mm(jnp.concatenate([rows, added.astype(BF)], 1), first) + bias
    hid = jnp.maximum(pre, 0.0).astype(BF)
    norm, rstd = normed(hid, second)
    return hid, norm, rstd


def layer_back(cot, hid, norm, rstd, first, second, gain):
    scaled = cot * gain
    along = jnp.mean(scaled * norm, 1, keepdims=True)
    cot_mixed = rstd * (scaled - jnp.mean(scaled, 1, keepdims=True) - norm * along)
    cot_hid = mm_nt(cot_mixed.astype(BF), second)
    cot_pre = jnp.where(hid.astype(F32) > 0, cot_hid, 0.0).astype(BF)
    return mm_nt(cot_pre, first)


def staged(first, second, between=None):
    first(0)

    def body(i, carry):
        if between is not None:
            between(i - 1)
        second(i - 1)
        first(i)
        return carry

    lax.fori_loop(1, STEPS, body, 0)
    second(STEPS - 1)


def rows_at(i):
    return pl.ds(i * CHUNK if isinstance(i, int) else pl.multiple_of(i * CHUNK, CHUNK), CHUNK)


def edge_forward(snd, rcv, lat, table, mixer, gain, norm_o, hid_o, rstd_o, code_o, sums, write, between):
    sums[...] = jnp.zeros_like(sums)

    def gather(i):
        sl = rows_at(i)
        s_rows, r_rows = id_code(snd[:, sl]).T, id_code(rcv[:, sl]).T
        code_o[sl, :] = r_rows
        pre = mm(jnp.concatenate([one_hots(s_rows, 6, 1), one_hots(r_rows, 4, 1), lat[sl, :]], 1), table[...])
        hid_o[sl, :] = jnp.maximum(pre[:, :L] + pre[:, L:], 0.0).astype(BF)

    def update(i):
        sl = rows_at(i)
        mixed = mm(hid_o[sl, :], mixer)
        center = mixed[:, :L] - mixed[:, L:]
        rstd = lax.rsqrt(mm((center * center).astype(BF), averager()) + eps)
        norm = center * rstd
        norm_o[sl, :] = norm.astype(BF)
        rstd_o[sl, :] = rstd.astype(BF)
        change = norm * gain
        write(i, sl, (lat[sl, :].astype(F32) + change).astype(BF))
        sums[...] += mm(one_hots(id_code(rcv[:, sl]), 4, 0), halves(change))

    staged(gather, update, between)


def edge_backward(
    snd, rcv, code_i, cot_table, cot, norm_i, hid_i, rstd_i, w_lat, second, gain, table_o, pre_o, write
):
    table_o[...] = jnp.zeros_like(table_o)

    def through(i):
        sl = rows_at(i)
        norm = norm_i[sl, :].astype(F32)
        scaled = (cot[sl, :].astype(F32) + mm(one_hots(code_i[sl, :], 4, 1), cot_table)) * gain
        along = mm((scaled * norm).astype(BF), averager())
        cot_mixed = (rstd_i[sl, :].astype(F32) * (scaled - norm * along)).astype(BF)
        cot_hid = mm_nt(cot_mixed, second)
        pre_o[sl, :] = jnp.where(hid_i[sl, :].astype(F32) > 0, cot_hid, 0.0).astype(BF)

    def spread(i):
        sl = rows_at(i)
        cot_pre = pre_o[sl, :]
        write(i, sl, (cot[sl, :].astype(F32) + mm_nt(cot_pre, w_lat)).astype(BF))
        hots = jnp.concatenate([one_hots(id_code(snd[:, sl]), 6, 0), one_hots(id_code(rcv[:, sl]), 4, 0)], 0)
        table_o[...] += mm(hots, cot_pre)

    staged(through, spread)


def kernel(*refs):
    sources, targets, rest = refs[:INPUTS], refs[INPUTS + 6 : 2 * INPUTS + 6], refs[2 * INPUTS + 6 :]
    (
        snd, rcv, chosen, own_dev, own_slot, lat, cot, fine, top, cot_fine, cot_top,
        e_first, e_bias, e_second, e_gain, n_first, n_bias, n_second, n_gain, c_first, c_bias, c_second, c_gain,
    ) = targets
    new_nodes_o, new_edges_o, new_coarse_o, grad_nodes_o, grad_edges_o, grad_coarse_o = refs[INPUTS : INPUTS + 6]
    (
        norm, hid, rstd, code, new_v, grad_v, cot_pre, table, sums, back_table, pick,
        mir_out, mir_in, early_out, early_in, mid_out, mid_in, grad_out, grad_in, row_out, row_in, ret_out, ret_in,
        load_sem, new_sem, grad_sem, mir_s, mir_r, ret_s, ret_r, early_s, early_r, mid_s, mid_r,
        gback_s, gback_r, row_s, row_r,
    ) = rest
    dom, slab = lax.axis_index("dom"), lax.axis_index("slab")
    me = dom * SLAB + slab

    loads = [pltpu.make_async_copy(src, dst, load_sem.at[k]) for k, (src, dst) in enumerate(zip(sources, targets))]
    for load in loads:
        load.start()

    def peers(act):
        def body(step, carry):
            other = lax.rem(me + step, DEVICES)
            act(other, (other // SLAB, lax.rem(other, SLAB)))
            return carry

        lax.fori_loop(1, DEVICES, body, 0)

    barrier = pltpu.get_barrier_semaphore()
    peers(lambda other, place: pl.semaphore_signal(barrier, inc=1, device_id=place, device_id_type=MESH))

    def exchange(out, land, send, recv):
        def start(other, place):
            pltpu.make_async_remote_copy(
                src_ref=out.at[other], dst_ref=land.at[me], send_sem=send, recv_sem=recv,
                device_id=place, device_id_type=MESH,
            ).start()

        peers(start)
        land[me] = out[me]

    def finish(out, land, send, recv):
        for ref, sem in ((land, recv), (out, send)):
            whole = ref.at[pl.ds(0, DEVICES - 1)]
            pltpu.make_async_copy(whole, whole, sem).wait()

    def blocks(wide):
        return wide.reshape(DEVICES, CAP, L)

    def rows_of(land):
        return land[...].astype(F32).reshape(DEVICES * CAP, L).astype(BF)

    below, above = (dom - 1, slab), (dom + 1, slab)
    left, right = (dom, slab - 1), (dom, slab + 1)
    has = {"below": dom > 0, "above": dom < DOM - 1, "left": slab > 0, "right": slab < SLAB - 1}
    spot = {"below": below, "above": above, "left": left, "right": right}

    def mirrors(out, land, send, recv, targets, sources):
        copies = [
            pltpu.make_async_remote_copy(
                src_ref=out.at[k], dst_ref=land.at[k], send_sem=send.at[k], recv_sem=recv.at[k],
                device_id=spot[targets[k]], device_id_type=MESH,
            )
            for k in range(4)
        ]
        for k in range(4):
            pl.when(has[targets[k]])(copies[k].start)
            pl.when(jnp.logical_not(has[sources[k]]))(lambda k=k: land.__setitem__(k, jnp.zeros((MIRROR, L), BF)))

        def wait():
            for k in range(4):
                pl.when(has[sources[k]])(copies[k].wait_recv)
                pl.when(has[targets[k]])(copies[k].wait_send)

        return wait

    for k, load in enumerate(loads):
        if k not in (5, 6):
            load.wait()

    picked = jnp.concatenate([chosen[k : k + 1, :] for k in range(4)], 1)
    chosen_code = id_code(picked)
    mir_out[...] = mm(one_hots(chosen_code.T, 4, 1), fine[...]).astype(BF).reshape(4, MIRROR, L)

    owner = own_dev[...]
    group = one_hots(id_code(owner), 1, 0)
    place = lax.broadcasted_iota(jnp.int32, (NODES, NODES), 0)
    earlier = jnp.where(place < lax.broadcasted_iota(jnp.int32, (NODES, NODES), 1), 1.0, 0.0).astype(BF)
    rank = jnp.sum(mm(group, earlier) * group.astype(F32), 0, keepdims=True)
    send_code = id_code(owner * CAP + rank.astype(jnp.int32))
    pick[...] = one_hots(send_code, CAP, 0)
    slot_rows = jnp.broadcast_to((own_slot[...] + 1).astype(F32).astype(BF), (L, NODES)).T
    early = mm(pick[...], jnp.concatenate([cot_fine[...], slot_rows], 1))
    early_out[...] = jnp.concatenate([blocks(early[:, :L]), blocks(early[:, L:])], 1).astype(BF)

    pl.semaphore_wait(barrier, DEVICES - 1)
    mirror_wait = mirrors(
        mir_out, mir_in, mir_s, mir_r, ("above", "below", "right", "left"), ("below", "above", "left", "right")
    )
    exchange(early_out, early_in, early_s, early_r)

    w_lat, w_src, w_tgt = e_first[:L, :], e_first[L : 2 * L, :], e_first[2 * L :, :]
    table[:NODES, :] = halves(mm(fine[...], w_src))
    table[6 * L : 10 * L, :] = halves(mm(fine[...], w_tgt) + e_bias[...])
    table[10 * L :, :] = jnp.concatenate([w_lat, jnp.zeros((L, L), BF)], 1)
    second = e_second[...].astype(F32)
    second_mean = jnp.broadcast_to(jnp.mean(second, 1, keepdims=True), (L, L))
    mixer = jnp.concatenate([e_second[...], second_mean.astype(BF)], 1)
    mirror_wait()
    table[NODES : 6 * L, :] = halves(mm(mir_in[...].reshape(4 * MIRROR, L), w_src))
    loads[5].wait()

    def write_new(i, sl, value):
        new_v[sl, :] = value
        pltpu.make_async_copy(new_v.at[sl], new_edges_o.at[sl], new_sem.at[i]).start()

    edge_forward(snd, rcv, lat, table, mixer, e_gain[...], norm, hid, rstd, code, sums, write_new, None)

    summed = sums[:, :L] + sums[:, L:]
    n_hid, n_norm, n_rstd = layer(fine[...], summed, n_first[...], n_bias[...], n_second[...])
    middle = (fine[...].astype(F32) + n_norm * n_gain[...]).astype(BF)
    mid_out[...] = blocks(mm(pick[...], middle)).astype(BF)
    exchange(mid_out, mid_in, mid_s, mid_r)

    finish(early_out, early_in, early_s, early_r)
    early_rows = early_in[...].astype(F32)
    slots = early_rows[:, CAP:].reshape(DEVICES * CAP, L)
    lane = lax.broadcasted_iota(jnp.int32, (DEVICES * CAP, L), 1).astype(F32)
    held = jnp.where(slots == lane + 1.0, 1.0, 0.0).astype(BF)
    gather = held.T
    cot_at = mm(gather, early_rows[:, :CAP].reshape(DEVICES * CAP, L).astype(BF))
    cot_new = (cot_top[...].astype(F32) + cot_at.astype(BF).astype(F32)).astype(BF).astype(F32)
    finish(mid_out, mid_in, mid_s, mid_r)
    pooled = mm(gather, rows_of(mid_in))
    c_hid, c_norm, c_rstd = layer(top[...], pooled, c_first[...], c_bias[...], c_second[...])
    new_top = (top[...].astype(F32) + c_norm * c_gain[...]).astype(BF)
    c_back = layer_back(cot_new, c_hid, c_norm, c_rstd, c_first[...], c_second[...], c_gain[...])
    grad_out[...] = blocks(mm(held, c_back[:, L:].astype(BF))).astype(BF)
    exchange(grad_out, grad_in, gback_s, gback_r)
    row_out[...] = blocks(mm(held, new_top)).astype(BF)
    exchange(row_out, row_in, row_s, row_r)
    new_coarse_o[...] = new_top
    grad_coarse_o[...] = cot_new + c_back[:, :L]

    second_c = (second - second_mean).astype(BF)
    loads[6].wait()
    finish(grad_out, grad_in, gback_s, gback_r)
    reply = one_hots(send_code.T, CAP, 1)
    cot_mid = (cot_fine[...].astype(F32) + mm(reply, rows_of(grad_in))).astype(BF).astype(F32)
    n_back = layer_back(cot_mid, n_hid, n_norm, n_rstd, n_first[...], n_second[...], n_gain[...])

    def write_grad(i, sl, value):
        grad_v[sl, :] = value
        pltpu.make_async_copy(grad_v.at[sl], grad_edges_o.at[sl], grad_sem.at[i]).start()

    edge_backward(
        snd, rcv, code, n_back[:, L:].astype(BF), cot, norm, hid, rstd, w_lat, second_c, e_gain[...],
        back_table, cot_pre, write_grad,
    )
    back = mm_nt(back_table[NODES : 6 * L, :].astype(BF), w_src)
    ret_out[...] = back.astype(BF).reshape(4, MIRROR, L)
    return_wait = mirrors(
        ret_out, ret_in, ret_s, ret_r, ("below", "above", "left", "right"), ("above", "below", "right", "left")
    )
    total = cot_mid + n_back[:, :L] + mm_nt(back_table[:NODES, :].astype(BF), w_src)
    total = total + mm_nt(back_table[6 * L :, :].astype(BF), w_tgt)
    finish(row_out, row_in, row_s, row_r)
    new_nodes_o[...] = (middle.astype(F32) + mm(reply, rows_of(row_in))).astype(BF)
    return_wait()
    grad_nodes_o[...] = total + mm(one_hots(chosen_code, 4, 0), ret_in[...].reshape(4 * MIRROR, L))
    for i in range(STEPS):
        sl = pl.ds(i * CHUNK, CHUNK)
        pltpu.make_async_copy(new_v.at[sl], new_edges_o.at[sl], new_sem.at[i]).wait()
        pltpu.make_async_copy(grad_v.at[sl], grad_edges_o.at[sl], grad_sem.at[i]).wait()


def finish_kernel(*refs):
    ins, outs, held, (wide, load_sems, sems) = refs[:6], refs[6:12], refs[12:18], refs[18:]
    work = []
    for k in (4, 1, 0, 3, 2, 5):
        rows = ins[k].shape[0]
        count = PARTS if rows == EDGES else 1
        for i in range(count):
            sl = pl.ds(i * (rows // count), rows // count)
            n = len(work)
            final = wide if k == 4 else held[k]
            work.append((
                k, sl,
                pltpu.make_async_copy(ins[k].at[sl], held[k].at[sl], load_sems.at[n]),
                pltpu.make_async_copy(final.at[sl], outs[k].at[sl], sems.at[n]),
            ))
    for k, sl, load, store in work:
        load.start()
    for k, sl, load, store in work:
        load.wait()
        if k == 4:
            wide[sl, :] = held[k][sl, :].astype(F32)
        store.start()
    for k, sl, load, store in work:
        store.wait()


VM = pl.BlockSpec(memory_space=pltpu.VMEM)
HBM = pl.BlockSpec(memory_space=pltpu.HBM)
ANY = pl.BlockSpec(memory_space=pl.ANY)


def shaped(*sizes, dtype=BF):
    return jax.ShapeDtypeStruct(sizes, dtype)


def local(
    nodes, edges, coarse, senders, receivers, mirror_rows, owner_device, owner_slot,
    edge_first, edge_bias, edge_second, edge_gain, node_first, node_bias, node_second, node_gain,
    coarse_first, coarse_bias, coarse_second, coarse_gain, cot_nodes, cot_edges, cot_coarse,
):
    def line(v):
        return v.reshape(1, -1)

    edge_rows = [pltpu.VMEM((EDGES, L), BF)] * 7
    pair = lambda *sizes: [pltpu.VMEM(sizes, BF)] * 2
    dma = pltpu.SemaphoreType.DMA
    ins = (
        line(senders), line(receivers), mirror_rows[0, 0], line(owner_device), line(owner_slot),
        edges[0, 0], cot_edges[0, 0], nodes[0, 0], coarse[0, 0], cot_nodes[0, 0], cot_coarse[0, 0],
        edge_first, line(edge_bias), edge_second, line(edge_gain),
        node_first, line(node_bias), node_second, line(node_gain),
        coarse_first, line(coarse_bias), coarse_second, line(coarse_gain),
    )
    outs = pl.pallas_call(
        kernel,
        out_shape=[
            shaped(NODES, L), shaped(EDGES, L), shaped(128, L),
            shaped(NODES, L, dtype=F32), shaped(EDGES, L), shaped(128, L, dtype=F32),
        ],
        in_specs=[HBM] * INPUTS,
        out_specs=[VM, HBM, VM, VM, HBM, VM],
        scratch_shapes=[pltpu.VMEM(v.shape, v.dtype) for v in ins]
        + edge_rows
        + [
            pltpu.VMEM((11 * L, 2 * L), BF), pltpu.VMEM((NODES, 2 * L), F32), pltpu.VMEM((10 * L, L), F32),
            pltpu.VMEM((DEVICES * CAP, NODES), BF),
        ]
        + pair(4, MIRROR, L) + pair(DEVICES, 2 * CAP, L) + pair(DEVICES, CAP, L) * 3 + pair(4, MIRROR, L)
        + [dma((INPUTS,)), dma((STEPS,)), dma((STEPS,))] + [dma((4,))] * 4 + [dma] * 8,
        compiler_params=pltpu.CompilerParams(
            vmem_limit_bytes=58 << 20, collective_id=0, has_side_effects=True
        ),
        name="mesh_layer",
    )(*ins)
    outs = pl.pallas_call(
        finish_kernel,
        out_shape=[
            shaped(NODES, L), shaped(EDGES, L), shaped(128, L),
            shaped(NODES, L, dtype=F32), shaped(EDGES, L, dtype=F32), shaped(128, L, dtype=F32),
        ],
        in_specs=[HBM] * 6,
        out_specs=[HBM] * 6,
        scratch_shapes=[pltpu.VMEM(v.shape, v.dtype) for v in outs]
        + [pltpu.VMEM((EDGES, L), F32)] + [dma((2 * PARTS + 4,))] * 2,
        compiler_params=pltpu.CompilerParams(vmem_limit_bytes=58 << 20),
        name="write_results",
    )(*outs)
    return tuple(o[None, None] for o in outs)


def solution(mesh):
    four, three, whole = P("dom", "slab", None, None), P("dom", "slab", None), P()
    in_specs = (four, four, four, three, three, four, four, three) + (whole,) * 12 + (four,) * 3
    return jax.shard_map(local, mesh=mesh, in_specs=in_specs, out_specs=(four,) * 6, check_vma=False)
```

```python
import functools

import jax
import jax.numpy as jnp
from jax import lax
from jax.experimental import pallas as pl
from jax.experimental.pallas import tpu as pltpu
from jax.sharding import PartitionSpec as P

eps = 1e-05
BF = jnp.bfloat16
F32 = jnp.float32
MESH = pl.DeviceIdType.MESH
DOM, SLAB, DEVICES = 8, 16, 128
NODES, EDGES, MIRROR, CAP, L = 512, 8192, 64, 8, 128
CHUNK = 2048
STEPS = EDGES // CHUNK
PARTS = 4
INPUTS = 23
FIRST = (7, 2, 3, 4, 9)
LAST = (5, 6)
S_HALF, R_HALF = 384, 256


def mm(a, b):
    return lax.dot_general(a, b, (((1,), (0,)), ((), ())), preferred_element_type=F32)


def mm_nt(a, b):
    return lax.dot_general(a, b, (((1,), (1,)), ((), ())), preferred_element_type=F32)


def averager():
    return jnp.full((L, L), 1.0 / L, BF)


def id_code(row):
    n = row.shape[1]
    low = jnp.broadcast_to((row & 127).astype(F32).astype(BF), (128, n))
    high = jnp.broadcast_to((row >> 7).astype(F32).astype(BF), (128, n))
    place = lax.broadcasted_iota(jnp.int32, (128, n), 0).astype(F32).astype(BF)
    return jnp.where(low == place, high, BF(-1))


def one_hots(code, blocks, axis):
    return jnp.concatenate([jnp.where(code == BF(k), BF(1), BF(0)) for k in range(blocks)], axis)


def halves(x):
    high = x.astype(BF)
    return jnp.concatenate([high, (x - high.astype(F32)).astype(BF)], 1)


def normed(hid, second):
    mixed = mm(hid, second)
    center = mixed - jnp.mean(mixed, 1, keepdims=True)
    rstd = lax.rsqrt(jnp.mean(center * center, 1, keepdims=True) + eps)
    return center * rstd, rstd


def layer(rows, added, first, bias, second):
    pre = mm(jnp.concatenate([rows, added.astype(BF)], 1), first) + bias
    hid = jnp.maximum(pre, 0.0).astype(BF)
    norm, rstd = normed(hid, second)
    return hid, norm, rstd


def layer_back(cot, hid, norm, rstd, first, second, gain):
    scaled = cot * gain
    along = jnp.mean(scaled * norm, 1, keepdims=True)
    cot_mixed = rstd * (scaled - jnp.mean(scaled, 1, keepdims=True) - norm * along)
    cot_hid = mm_nt(cot_mixed.astype(BF), second)
    cot_pre = jnp.where(hid.astype(F32) > 0, cot_hid, 0.0).astype(BF)
    return mm_nt(cot_pre, first)


def staged(first, second, between=None):
    first(0)

    def body(i, carry):
        if between is not None:
            between(i - 1)
        second(i - 1)
        first(i)
        return carry

    lax.fori_loop(1, STEPS, body, 0)
    second(STEPS - 1)


def rows_at(i):
    return pl.ds(i * CHUNK if isinstance(i, int) else pl.multiple_of(i * CHUNK, CHUNK), CHUNK)


def edge_forward(snd, rcv, lat, table, mixer, gain, norm_o, hid_o, rstd_o, sums, write, between):
    sums[...] = jnp.zeros_like(sums)

    def gather(i):
        sl = rows_at(i)
        s_rows, r_rows = id_code(snd[:, sl]).T, id_code(rcv[:, sl]).T
        pre = mm(jnp.concatenate([one_hots(s_rows, 6, 1), one_hots(r_rows, 4, 1), lat[sl, :]], 1), table[...])
        hid_o[sl, :] = jnp.maximum(pre[:, :L] + pre[:, L:], 0.0).astype(BF)

    def update(i):
        sl = rows_at(i)
        mixed = mm(hid_o[sl, :], mixer)
        center = mixed[:, :L] - mixed[:, L:]
        rstd = lax.rsqrt(jnp.mean(center * center, 1, keepdims=True) + eps)
        norm = center * rstd
        norm_o[sl, :] = norm.astype(BF)
        rstd_o[sl, :] = jnp.broadcast_to(rstd, norm.shape).astype(BF)
        change = norm * gain
        write(i, sl, (lat[sl, :].astype(F32) + change).astype(BF))
        sums[...] += mm(one_hots(id_code(rcv[:, sl]), 4, 0), halves(change))

    staged(gather, update, between)


def edge_prepare(snd, rcv, code_o, s_upper, r_upper):
    def body(i, carry):
        sl = rows_at(i)
        for ids, half, upper in ((snd, S_HALF, s_upper), (rcv, R_HALF, r_upper)):
            flag = jnp.where(ids[:, sl] >= half, 1.0, 0.0).astype(BF)
            upper[sl, :] = jnp.broadcast_to(flag, (L, CHUNK)).T
        code_o[sl, :] = id_code(within(rcv[:, sl], R_HALF)).T
        return carry

    lax.fori_loop(0, STEPS, body, 0)


def within(ids, half):
    return jnp.where(ids >= half, ids - half, ids)


def beside(rows):
    half = rows.shape[0] // 2
    return jnp.concatenate([rows[:half], rows[half:]], 1)


def below_each_other(pair):
    return jnp.concatenate([pair[:, :L], pair[:, L:]], 0)


def parted(rows, upper):
    chosen = upper > BF(0)
    return jnp.concatenate([jnp.where(chosen, BF(0), rows), jnp.where(chosen, rows, BF(0))], 1)


def edge_backward(
    snd, rcv, code_i, s_upper, r_upper, cot_table, cot, norm_i, hid_i, rstd_i, w_lat, second, gain,
    s_table, r_table, pre_o, write,
):
    s_table[...] = jnp.zeros_like(s_table)
    r_table[...] = jnp.zeros_like(r_table)

    def through(i):
        sl = rows_at(i)
        norm = norm_i[sl, :].astype(F32)
        found = mm(one_hots(code_i[sl, :], 2, 1), cot_table)
        found = jnp.where(r_upper[sl, :].astype(F32) > 0, found[:, L:], found[:, :L])
        scaled = (cot[sl, :].astype(F32) + found) * gain
        along = mm((scaled * norm).astype(BF), averager())
        cot_mixed = (rstd_i[sl, :].astype(F32) * (scaled - norm * along)).astype(BF)
        cot_hid = mm_nt(cot_mixed, second)
        pre_o[sl, :] = jnp.where(hid_i[sl, :].astype(F32) > 0, cot_hid, 0.0).astype(BF)

    def spread(i):
        sl = rows_at(i)
        cot_pre = pre_o[sl, :]
        write(i, sl, (cot[sl, :].astype(F32) + mm_nt(cot_pre, w_lat)).astype(BF))
        s_code, r_code = id_code(within(snd[:, sl], S_HALF)), id_code(within(rcv[:, sl], R_HALF))
        s_table[...] += mm(one_hots(s_code, 3, 0), parted(cot_pre, s_upper[sl, :]))
        r_table[...] += mm(one_hots(r_code, 2, 0), parted(cot_pre, r_upper[sl, :]))

    staged(through, spread)


def kernel(*refs):
    sources, targets, rest = refs[:INPUTS], refs[INPUTS + 6 : 2 * INPUTS + 6], refs[2 * INPUTS + 6 :]
    (
        snd, rcv, chosen, own_dev, own_slot, lat, cot, fine, top, cot_fine, cot_top,
        e_first, e_bias, e_second, e_gain, n_first, n_bias, n_second, n_gain, c_first, c_bias, c_second, c_gain,
    ) = targets
    new_nodes_o, new_edges_o, new_coarse_o, grad_nodes_o, grad_edges_o, grad_coarse_o = refs[INPUTS : INPUTS + 6]
    (
        norm, hid, rstd, code, new_v, grad_v, cot_pre, s_upper, r_upper, table, sums, s_table, r_table, pick,
        mir_out, mir_in, early_out, early_in, mid_out, mid_in, grad_out, grad_in, row_out, row_in, ret_out, ret_in,
        load_sem, new_sem, grad_sem, mir_s, mir_r, ret_s, ret_r, early_s, early_r, mid_s, mid_r,
        gback_s, gback_r, row_s, row_r,
    ) = rest
    dom, slab = lax.axis_index("dom"), lax.axis_index("slab")
    me = dom * SLAB + slab

    loads = [pltpu.make_async_copy(src, dst, load_sem.at[k]) for k, (src, dst) in enumerate(zip(sources, targets))]
    for k in FIRST + tuple(k for k in range(INPUTS) if k not in FIRST + LAST) + LAST:
        loads[k].start()

    def peers(act):
        def body(step, carry):
            other = lax.rem(me + step, DEVICES)
            act(other, (other // SLAB, lax.rem(other, SLAB)))
            return carry

        lax.fori_loop(1, DEVICES, body, 0)

    barrier = pltpu.get_barrier_semaphore()
    peers(lambda other, place: pl.semaphore_signal(barrier, inc=1, device_id=place, device_id_type=MESH))

    def exchange(out, land, send, recv):
        def start(other, place):
            pltpu.make_async_remote_copy(
                src_ref=out.at[other], dst_ref=land.at[me], send_sem=send, recv_sem=recv,
                device_id=place, device_id_type=MESH,
            ).start()

        peers(start)
        land[me] = out[me]

    def finish(out, land, send, recv):
        for ref, sem in ((land, recv), (out, send)):
            whole = ref.at[pl.ds(0, DEVICES - 1)]
            pltpu.make_async_copy(whole, whole, sem).wait()

    def blocks(wide):
        return wide.reshape(DEVICES, CAP, L)

    def rows_of(land):
        return land[...].astype(F32).reshape(DEVICES * CAP, L).astype(BF)

    below, above = (dom - 1, slab), (dom + 1, slab)
    left, right = (dom, slab - 1), (dom, slab + 1)
    has = {"below": dom > 0, "above": dom < DOM - 1, "left": slab > 0, "right": slab < SLAB - 1}
    spot = {"below": below, "above": above, "left": left, "right": right}

    def mirrors(out, land, send, recv, targets, sources):
        copies = [
            pltpu.make_async_remote_copy(
                src_ref=out.at[k], dst_ref=land.at[k], send_sem=send.at[k], recv_sem=recv.at[k],
                device_id=spot[targets[k]], device_id_type=MESH,
            )
            for k in range(4)
        ]
        for k in range(4):
            pl.when(has[targets[k]])(copies[k].start)
            pl.when(jnp.logical_not(has[sources[k]]))(lambda k=k: land.__setitem__(k, jnp.zeros((MIRROR, L), BF)))

        def wait():
            for k in range(4):
                pl.when(has[sources[k]])(copies[k].wait_recv)
                pl.when(has[targets[k]])(copies[k].wait_send)

        return wait

    for k, load in enumerate(loads):
        if k not in (5, 6):
            load.wait()

    picked = jnp.concatenate([chosen[k : k + 1, :] for k in range(4)], 1)
    chosen_code = id_code(picked)
    mir_out[...] = mm(one_hots(chosen_code.T, 4, 1), fine[...]).astype(BF).reshape(4, MIRROR, L)

    pl.semaphore_wait(barrier, DEVICES - 1)
    mirror_wait = mirrors(
        mir_out, mir_in, mir_s, mir_r, ("above", "below", "right", "left"), ("below", "above", "left", "right")
    )

    owner = own_dev[...]
    group = one_hots(id_code(owner), 1, 0)
    place = lax.broadcasted_iota(jnp.int32, (NODES, NODES), 0)
    earlier = jnp.where(place < lax.broadcasted_iota(jnp.int32, (NODES, NODES), 1), 1.0, 0.0).astype(BF)
    rank = jnp.sum(mm(group, earlier) * group.astype(F32), 0, keepdims=True)
    send_code = id_code(owner * CAP + rank.astype(jnp.int32))
    pick[...] = one_hots(send_code, CAP, 0)
    slot_rows = jnp.broadcast_to((own_slot[...] + 1).astype(F32).astype(BF), (L, NODES)).T
    early = mm(pick[...], jnp.concatenate([cot_fine[...], slot_rows], 1))
    early_out[...] = jnp.concatenate([blocks(early[:, :L]), blocks(early[:, L:])], 1).astype(BF)
    exchange(early_out, early_in, early_s, early_r)

    w_lat, w_src, w_tgt = e_first[:L, :], e_first[L : 2 * L, :], e_first[2 * L :, :]
    table[:NODES, :] = halves(mm(fine[...], w_src))
    table[6 * L : 10 * L, :] = halves(mm(fine[...], w_tgt) + e_bias[...])
    table[10 * L :, :] = jnp.concatenate([w_lat, jnp.zeros((L, L), BF)], 1)
    second = e_second[...].astype(F32)
    second_mean = jnp.broadcast_to(jnp.mean(second, 1, keepdims=True), (L, L))
    mixer = jnp.concatenate([e_second[...], second_mean.astype(BF)], 1)
    mirror_wait()
    table[NODES : 6 * L, :] = halves(mm(mir_in[...].reshape(4 * MIRROR, L), w_src))
    loads[5].wait()

    def write_new(i, sl, value):
        new_v[sl, :] = value
        pltpu.make_async_copy(new_v.at[sl], new_edges_o.at[sl], new_sem.at[i]).start()

    edge_forward(snd, rcv, lat, table, mixer, e_gain[...], norm, hid, rstd, sums, write_new, None)

    summed = sums[:, :L] + sums[:, L:]
    n_hid, n_norm, n_rstd = layer(fine[...], summed, n_first[...], n_bias[...], n_second[...])
    middle = (fine[...].astype(F32) + n_norm * n_gain[...]).astype(BF)
    mid_out[...] = blocks(mm(pick[...], middle)).astype(BF)
    exchange(mid_out, mid_in, mid_s, mid_r)
    edge_prepare(snd, rcv, code, s_upper, r_upper)

    finish(early_out, early_in, early_s, early_r)
    early_rows = early_in[...].astype(F32)
    slots = early_rows[:, CAP:].reshape(DEVICES * CAP, L)
    lane = lax.broadcasted_iota(jnp.int32, (DEVICES * CAP, L), 1).astype(F32)
    held = jnp.where(slots == lane + 1.0, 1.0, 0.0).astype(BF)
    gather = held.T
    cot_at = mm(gather, early_rows[:, :CAP].reshape(DEVICES * CAP, L).astype(BF))
    cot_new = (cot_top[...].astype(F32) + cot_at.astype(BF).astype(F32)).astype(BF).astype(F32)
    finish(mid_out, mid_in, mid_s, mid_r)
    pooled = mm(gather, rows_of(mid_in))
    c_hid, c_norm, c_rstd = layer(top[...], pooled, c_first[...], c_bias[...], c_second[...])
    new_top = (top[...].astype(F32) + c_norm * c_gain[...]).astype(BF)
    c_back = layer_back(cot_new, c_hid, c_norm, c_rstd, c_first[...], c_second[...], c_gain[...])
    grad_out[...] = blocks(mm(held, c_back[:, L:].astype(BF))).astype(BF)
    exchange(grad_out, grad_in, gback_s, gback_r)
    row_out[...] = blocks(mm(held, new_top)).astype(BF)
    exchange(row_out, row_in, row_s, row_r)
    new_coarse_o[...] = new_top
    grad_coarse_o[...] = cot_new + c_back[:, :L]

    second_c = (second - second_mean).astype(BF)
    loads[6].wait()
    finish(grad_out, grad_in, gback_s, gback_r)
    reply = one_hots(send_code.T, CAP, 1)
    cot_mid = (cot_fine[...].astype(F32) + mm(reply, rows_of(grad_in))).astype(BF).astype(F32)
    n_back = layer_back(cot_mid, n_hid, n_norm, n_rstd, n_first[...], n_second[...], n_gain[...])

    def write_grad(i, sl, value):
        grad_v[sl, :] = value
        pltpu.make_async_copy(grad_v.at[sl], grad_edges_o.at[sl], grad_sem.at[i]).start()

    edge_backward(
        snd, rcv, code, s_upper, r_upper, beside(n_back[:, L:].astype(BF)), cot, norm, hid, rstd,
        w_lat, second_c, e_gain[...], s_table, r_table, cot_pre, write_grad,
    )
    back_table = below_each_other(s_table[...]).astype(BF)
    back = mm_nt(back_table[NODES:], w_src)
    ret_out[...] = back.astype(BF).reshape(4, MIRROR, L)
    return_wait = mirrors(
        ret_out, ret_in, ret_s, ret_r, ("below", "above", "left", "right"), ("above", "below", "right", "left")
    )
    total = cot_mid + n_back[:, :L] + mm_nt(back_table[:NODES], w_src)
    total = total + mm_nt(below_each_other(r_table[...]).astype(BF), w_tgt)
    finish(row_out, row_in, row_s, row_r)
    new_nodes_o[...] = (middle.astype(F32) + mm(reply, rows_of(row_in))).astype(BF)
    return_wait()
    grad_nodes_o[...] = total + mm(one_hots(chosen_code, 4, 0), ret_in[...].reshape(4 * MIRROR, L))
    for i in range(STEPS):
        sl = pl.ds(i * CHUNK, CHUNK)
        pltpu.make_async_copy(new_v.at[sl], new_edges_o.at[sl], new_sem.at[i]).wait()
        pltpu.make_async_copy(grad_v.at[sl], grad_edges_o.at[sl], grad_sem.at[i]).wait()


def finish_kernel(*refs):
    ins, outs, held, (wide, load_sems, sems) = refs[:6], refs[6:12], refs[12:18], refs[18:]
    work = []
    for k in (4, 1, 0, 3, 2, 5):
        rows = ins[k].shape[0]
        count = PARTS if rows == EDGES else 1
        for i in range(count):
            sl = pl.ds(i * (rows // count), rows // count)
            n = len(work)
            final = wide if k == 4 else held[k]
            work.append((
                k, sl,
                pltpu.make_async_copy(ins[k].at[sl], held[k].at[sl], load_sems.at[n]),
                pltpu.make_async_copy(final.at[sl], outs[k].at[sl], sems.at[n]),
            ))
    for k, sl, load, store in work:
        load.start()
    for k, sl, load, store in work:
        load.wait()
        if k == 4:
            wide[sl, :] = held[k][sl, :].astype(F32)
        store.start()
    for k, sl, load, store in work:
        store.wait()


VM = pl.BlockSpec(memory_space=pltpu.VMEM)
HBM = pl.BlockSpec(memory_space=pltpu.HBM)
ANY = pl.BlockSpec(memory_space=pl.ANY)


def shaped(*sizes, dtype=BF):
    return jax.ShapeDtypeStruct(sizes, dtype)


def local(
    nodes, edges, coarse, senders, receivers, mirror_rows, owner_device, owner_slot,
    edge_first, edge_bias, edge_second, edge_gain, node_first, node_bias, node_second, node_gain,
    coarse_first, coarse_bias, coarse_second, coarse_gain, cot_nodes, cot_edges, cot_coarse,
):
    def line(v):
        return v.reshape(1, -1)

    edge_rows = [pltpu.VMEM((EDGES, L), BF)] * 9
    pair = lambda *sizes: [pltpu.VMEM(sizes, BF)] * 2
    dma = pltpu.SemaphoreType.DMA
    ins = (
        line(senders), line(receivers), mirror_rows[0, 0], line(owner_device), line(owner_slot),
        edges[0, 0], cot_edges[0, 0], nodes[0, 0], coarse[0, 0], cot_nodes[0, 0], cot_coarse[0, 0],
        edge_first, line(edge_bias), edge_second, line(edge_gain),
        node_first, line(node_bias), node_second, line(node_gain),
        coarse_first, line(coarse_bias), coarse_second, line(coarse_gain),
    )
    outs = pl.pallas_call(
        kernel,
        out_shape=[
            shaped(NODES, L), shaped(EDGES, L), shaped(128, L),
            shaped(NODES, L, dtype=F32), shaped(EDGES, L), shaped(128, L, dtype=F32),
        ],
        in_specs=[HBM] * INPUTS,
        out_specs=[VM, HBM, VM, VM, HBM, VM],
        scratch_shapes=[pltpu.VMEM(v.shape, v.dtype) for v in ins]
        + edge_rows
        + [
            pltpu.VMEM((11 * L, 2 * L), BF), pltpu.VMEM((NODES, 2 * L), F32), pltpu.VMEM((S_HALF, 2 * L), F32),
            pltpu.VMEM((R_HALF, 2 * L), F32),
            pltpu.VMEM((DEVICES * CAP, NODES), BF),
        ]
        + pair(4, MIRROR, L) + pair(DEVICES, 2 * CAP, L) + pair(DEVICES, CAP, L) * 3 + pair(4, MIRROR, L)
        + [dma((INPUTS,)), dma((STEPS,)), dma((STEPS,))] + [dma((4,))] * 4 + [dma] * 8,
        compiler_params=pltpu.CompilerParams(
            vmem_limit_bytes=58 << 20, collective_id=0, has_side_effects=True
        ),
        name="mesh_layer",
    )(*ins)
    outs = pl.pallas_call(
        finish_kernel,
        out_shape=[
            shaped(NODES, L), shaped(EDGES, L), shaped(128, L),
            shaped(NODES, L, dtype=F32), shaped(EDGES, L, dtype=F32), shaped(128, L, dtype=F32),
        ],
        in_specs=[HBM] * 6,
        out_specs=[HBM] * 6,
        scratch_shapes=[pltpu.VMEM(v.shape, v.dtype) for v in outs]
        + [pltpu.VMEM((EDGES, L), F32)] + [dma((2 * PARTS + 4,))] * 2,
        compiler_params=pltpu.CompilerParams(vmem_limit_bytes=58 << 20),
        name="write_results",
    )(*outs)
    return tuple(o[None, None] for o in outs)


def solution(mesh):
    four, three, whole = P("dom", "slab", None, None), P("dom", "slab", None), P()
    in_specs = (four, four, four, three, three, four, four, three) + (whole,) * 12 + (four,) * 3
    return jax.shard_map(local, mesh=mesh, in_specs=in_specs, out_specs=(four,) * 6, check_vma=False)
```

```python
import functools

import jax
import jax.numpy as jnp
from jax import lax
from jax.experimental import pallas as pl
from jax.experimental.pallas import tpu as pltpu
from jax.sharding import PartitionSpec as P

eps = 1e-05
BF = jnp.bfloat16
F32 = jnp.float32
MESH = pl.DeviceIdType.MESH
DOM, SLAB, DEVICES = 8, 16, 128
NODES, EDGES, MIRROR, CAP, L = 512, 8192, 64, 8, 128
CHUNK = 2048
STEPS = EDGES // CHUNK
PARTS = 4
INPUTS = 23
FIRST = (7, 2, 3, 4, 9)
LAST = (5, 6)
S_HALF, R_HALF = 384, 256


def mm(a, b):
    return lax.dot_general(a, b, (((1,), (0,)), ((), ())), preferred_element_type=F32)


def mm_nt(a, b):
    return lax.dot_general(a, b, (((1,), (1,)), ((), ())), preferred_element_type=F32)


def averager():
    return jnp.full((L, L), 1.0 / L, BF)


def id_code(row):
    n = row.shape[1]
    low = jnp.broadcast_to((row & 127).astype(F32).astype(BF), (128, n))
    high = jnp.broadcast_to((row >> 7).astype(F32).astype(BF), (128, n))
    place = lax.broadcasted_iota(jnp.int32, (128, n), 0).astype(F32).astype(BF)
    return jnp.where(low == place, high, BF(-1))


def one_hots(code, blocks, axis):
    return jnp.concatenate([jnp.where(code == BF(k), BF(1), BF(0)) for k in range(blocks)], axis)


def halves(x):
    high = x.astype(BF)
    return jnp.concatenate([high, (x - high.astype(F32)).astype(BF)], 1)


def normed(hid, second):
    mixed = mm(hid, second)
    center = mixed - jnp.mean(mixed, 1, keepdims=True)
    rstd = lax.rsqrt(jnp.mean(center * center, 1, keepdims=True) + eps)
    return center * rstd, rstd


def layer(rows, added, first, bias, second):
    pre = mm(jnp.concatenate([rows, added.astype(BF)], 1), first) + bias
    hid = jnp.maximum(pre, 0.0).astype(BF)
    norm, rstd = normed(hid, second)
    return hid, norm, rstd


def layer_back(cot, hid, norm, rstd, first, second, gain):
    scaled = cot * gain
    along = jnp.mean(scaled * norm, 1, keepdims=True)
    cot_mixed = rstd * (scaled - jnp.mean(scaled, 1, keepdims=True) - norm * along)
    cot_hid = mm_nt(cot_mixed.astype(BF), second)
    cot_pre = jnp.where(hid.astype(F32) > 0, cot_hid, 0.0).astype(BF)
    return mm_nt(cot_pre, first)


def staged(first, second, between=None):
    first(0)

    def body(i, carry):
        if between is not None:
            between(i - 1)
        second(i - 1)
        first(i)
        return carry

    lax.fori_loop(1, STEPS, body, 0)
    second(STEPS - 1)


def rows_at(i):
    return pl.ds(i * CHUNK if isinstance(i, int) else pl.multiple_of(i * CHUNK, CHUNK), CHUNK)


def edge_forward(
    snd, rcv, lat, s_side, r_side, first, bias, mixer, gain, norm_o, hid_o, rstd_o, code_o, s_upper, r_upper, sums, write, between
):
    sums[...] = jnp.zeros_like(sums)

    def gather(i):
        sl = rows_at(i)
        for ids, half, upper in ((snd, S_HALF, s_upper), (rcv, R_HALF, r_upper)):
            flag = jnp.where(ids[:, sl] >= half, 1.0, 0.0).astype(BF)
            upper[sl, :] = jnp.broadcast_to(flag, (L, CHUNK)).T
        s_rows, r_rows = id_code(within(snd[:, sl], S_HALF)).T, id_code(within(rcv[:, sl], R_HALF)).T
        code_o[sl, :] = r_rows
        src, tgt = mm(one_hots(s_rows, 3, 1), s_side[...]), mm(one_hots(r_rows, 2, 1), r_side[...])
        src = jnp.where(s_upper[sl, :].astype(F32) > 0, src[:, L:], src[:, :L]).astype(BF)
        tgt = jnp.where(r_upper[sl, :].astype(F32) > 0, tgt[:, L:], tgt[:, :L]).astype(BF)
        pre = mm(jnp.concatenate([lat[sl, :], src, tgt], 1), first) + bias
        hid_o[sl, :] = jnp.maximum(pre, 0.0).astype(BF)

    def update(i):
        sl = rows_at(i)
        mixed = mm(hid_o[sl, :], mixer)
        center = mixed[:, :L] - mixed[:, L:]
        rstd = lax.rsqrt(jnp.mean(center * center, 1, keepdims=True) + eps)
        norm = center * rstd
        norm_o[sl, :] = norm.astype(BF)
        rstd_o[sl, :] = jnp.broadcast_to(rstd, norm.shape).astype(BF)
        change = norm * gain
        write(i, sl, (lat[sl, :].astype(F32) + change).astype(BF))
        sums[...] += mm(one_hots(id_code(rcv[:, sl]), 4, 0), halves(change))

    staged(gather, update, between)


def within(ids, half):
    return jnp.where(ids >= half, ids - half, ids)


def beside(rows):
    half = rows.shape[0] // 2
    return jnp.concatenate([rows[:half], rows[half:]], 1)


def below_each_other(pair):
    return jnp.concatenate([pair[:, :L], pair[:, L:]], 0)


def parted(rows, upper):
    chosen = upper > BF(0)
    return jnp.concatenate([jnp.where(chosen, BF(0), rows), jnp.where(chosen, rows, BF(0))], 1)


def edge_backward(
    snd, rcv, code_i, s_upper, r_upper, cot_table, cot, norm_i, hid_i, rstd_i, w_lat, second, gain,
    s_table, r_table, pre_o, write,
):
    s_table[...] = jnp.zeros_like(s_table)
    r_table[...] = jnp.zeros_like(r_table)

    def through(i):
        sl = rows_at(i)
        norm = norm_i[sl, :].astype(F32)
        found = mm(one_hots(code_i[sl, :], 2, 1), cot_table)
        found = jnp.where(r_upper[sl, :].astype(F32) > 0, found[:, L:], found[:, :L])
        scaled = (cot[sl, :].astype(F32) + found) * gain
        along = mm((scaled * norm).astype(BF), averager())
        cot_mixed = (rstd_i[sl, :].astype(F32) * (scaled - norm * along)).astype(BF)
        cot_hid = mm_nt(cot_mixed, second)
        pre_o[sl, :] = jnp.where(hid_i[sl, :].astype(F32) > 0, cot_hid, 0.0).astype(BF)

    def spread(i):
        sl = rows_at(i)
        cot_pre = pre_o[sl, :]
        write(i, sl, (cot[sl, :].astype(F32) + mm_nt(cot_pre, w_lat)).astype(BF))
        s_code, r_code = id_code(within(snd[:, sl], S_HALF)), id_code(within(rcv[:, sl], R_HALF))
        s_table[...] += mm(one_hots(s_code, 3, 0), parted(cot_pre, s_upper[sl, :]))
        r_table[...] += mm(one_hots(r_code, 2, 0), parted(cot_pre, r_upper[sl, :]))

    staged(through, spread)


def kernel(*refs):
    sources, targets, rest = refs[:INPUTS], refs[INPUTS + 6 : 2 * INPUTS + 6], refs[2 * INPUTS + 6 :]
    (
        snd, rcv, chosen, own_dev, own_slot, lat, cot, fine, top, cot_fine, cot_top,
        e_first, e_bias, e_second, e_gain, n_first, n_bias, n_second, n_gain, c_first, c_bias, c_second, c_gain,
    ) = targets
    new_nodes_o, new_edges_o, new_coarse_o, grad_nodes_o, grad_edges_o, grad_coarse_o = refs[INPUTS : INPUTS + 6]
    (
        norm, hid, rstd, code, new_v, grad_v, cot_pre, s_upper, r_upper, s_side, r_side, sums, s_table, r_table, pick,
        mir_out, mir_in, early_out, early_in, mid_out, mid_in, grad_out, grad_in, row_out, row_in, ret_out, ret_in,
        load_sem, new_sem, grad_sem, mir_s, mir_r, ret_s, ret_r, early_s, early_r, mid_s, mid_r,
        gback_s, gback_r, row_s, row_r,
    ) = rest
    dom, slab = lax.axis_index("dom"), lax.axis_index("slab")
    me = dom * SLAB + slab

    loads = [pltpu.make_async_copy(src, dst, load_sem.at[k]) for k, (src, dst) in enumerate(zip(sources, targets))]
    for k in FIRST + tuple(k for k in range(INPUTS) if k not in FIRST + LAST) + LAST:
        loads[k].start()

    def peers(act):
        def body(step, carry):
            other = lax.rem(me + step, DEVICES)
            act(other, (other // SLAB, lax.rem(other, SLAB)))
            return carry

        lax.fori_loop(1, DEVICES, body, 0)

    barrier = pltpu.get_barrier_semaphore()
    peers(lambda other, place: pl.semaphore_signal(barrier, inc=1, device_id=place, device_id_type=MESH))

    def exchange(out, land, send, recv):
        def start(other, place):
            pltpu.make_async_remote_copy(
                src_ref=out.at[other], dst_ref=land.at[me], send_sem=send, recv_sem=recv,
                device_id=place, device_id_type=MESH,
            ).start()

        peers(start)
        land[me] = out[me]

    def finish(out, land, send, recv):
        for ref, sem in ((land, recv), (out, send)):
            whole = ref.at[pl.ds(0, DEVICES - 1)]
            pltpu.make_async_copy(whole, whole, sem).wait()

    def blocks(wide):
        return wide.reshape(DEVICES, CAP, L)

    def rows_of(land):
        return land[...].astype(F32).reshape(DEVICES * CAP, L).astype(BF)

    below, above = (dom - 1, slab), (dom + 1, slab)
    left, right = (dom, slab - 1), (dom, slab + 1)
    has = {"below": dom > 0, "above": dom < DOM - 1, "left": slab > 0, "right": slab < SLAB - 1}
    spot = {"below": below, "above": above, "left": left, "right": right}

    def mirrors(out, land, send, recv, targets, sources):
        copies = [
            pltpu.make_async_remote_copy(
                src_ref=out.at[k], dst_ref=land.at[k], send_sem=send.at[k], recv_sem=recv.at[k],
                device_id=spot[targets[k]], device_id_type=MESH,
            )
            for k in range(4)
        ]
        for k in range(4):
            pl.when(has[targets[k]])(copies[k].start)
            pl.when(jnp.logical_not(has[sources[k]]))(lambda k=k: land.__setitem__(k, jnp.zeros((MIRROR, L), BF)))

        def wait():
            for k in range(4):
                pl.when(has[sources[k]])(copies[k].wait_recv)
                pl.when(has[targets[k]])(copies[k].wait_send)

        return wait

    for k, load in enumerate(loads):
        if k not in (5, 6):
            load.wait()

    picked = jnp.concatenate([chosen[k : k + 1, :] for k in range(4)], 1)
    chosen_code = id_code(picked)
    mir_out[...] = mm(one_hots(chosen_code.T, 4, 1), fine[...]).astype(BF).reshape(4, MIRROR, L)

    pl.semaphore_wait(barrier, DEVICES - 1)
    mirror_wait = mirrors(
        mir_out, mir_in, mir_s, mir_r, ("above", "below", "right", "left"), ("below", "above", "left", "right")
    )

    owner = own_dev[...]
    group = one_hots(id_code(owner), 1, 0)
    place = lax.broadcasted_iota(jnp.int32, (NODES, NODES), 0)
    earlier = jnp.where(place < lax.broadcasted_iota(jnp.int32, (NODES, NODES), 1), 1.0, 0.0).astype(BF)
    rank = jnp.sum(mm(group, earlier) * group.astype(F32), 0, keepdims=True)
    send_code = id_code(owner * CAP + rank.astype(jnp.int32))
    pick[...] = one_hots(send_code, CAP, 0)
    slot_rows = jnp.broadcast_to((own_slot[...] + 1).astype(F32).astype(BF), (L, NODES)).T
    early = mm(pick[...], jnp.concatenate([cot_fine[...], slot_rows], 1))
    early_out[...] = jnp.concatenate([blocks(early[:, :L]), blocks(early[:, L:])], 1).astype(BF)
    exchange(early_out, early_in, early_s, early_r)

    w_lat, w_src, w_tgt = e_first[:L, :], e_first[L : 2 * L, :], e_first[2 * L :, :]
    r_side[...] = beside(fine[...])
    second = e_second[...].astype(F32)
    second_mean = jnp.broadcast_to(jnp.mean(second, 1, keepdims=True), (L, L))
    mixer = jnp.concatenate([e_second[...], second_mean.astype(BF)], 1)
    mirror_wait()
    s_side[...] = beside(jnp.concatenate([fine[...], mir_in[...].reshape(4 * MIRROR, L)], 0))
    loads[5].wait()

    def write_new(i, sl, value):
        new_v[sl, :] = value
        pltpu.make_async_copy(new_v.at[sl], new_edges_o.at[sl], new_sem.at[i]).start()

    edge_forward(
        snd, rcv, lat, s_side, r_side, e_first[...], e_bias[...], mixer, e_gain[...], norm, hid, rstd, code, s_upper, r_upper, sums, write_new, None
    )

    summed = sums[:, :L] + sums[:, L:]
    n_hid, n_norm, n_rstd = layer(fine[...], summed, n_first[...], n_bias[...], n_second[...])
    middle = (fine[...].astype(F32) + n_norm * n_gain[...]).astype(BF)
    mid_out[...] = blocks(mm(pick[...], middle)).astype(BF)
    exchange(mid_out, mid_in, mid_s, mid_r)

    finish(early_out, early_in, early_s, early_r)
    early_rows = early_in[...].astype(F32)
    slots = early_rows[:, CAP:].reshape(DEVICES * CAP, L)
    lane = lax.broadcasted_iota(jnp.int32, (DEVICES * CAP, L), 1).astype(F32)
    held = jnp.where(slots == lane + 1.0, 1.0, 0.0).astype(BF)
    gather = held.T
    cot_at = mm(gather, early_rows[:, :CAP].reshape(DEVICES * CAP, L).astype(BF))
    cot_new = (cot_top[...].astype(F32) + cot_at.astype(BF).astype(F32)).astype(BF).astype(F32)
    finish(mid_out, mid_in, mid_s, mid_r)
    pooled = mm(gather, rows_of(mid_in))
    c_hid, c_norm, c_rstd = layer(top[...], pooled, c_first[...], c_bias[...], c_second[...])
    new_top = (top[...].astype(F32) + c_norm * c_gain[...]).astype(BF)
    c_back = layer_back(cot_new, c_hid, c_norm, c_rstd, c_first[...], c_second[...], c_gain[...])
    grad_out[...] = blocks(mm(held, c_back[:, L:].astype(BF))).astype(BF)
    exchange(grad_out, grad_in, gback_s, gback_r)
    row_out[...] = blocks(mm(held, new_top)).astype(BF)
    exchange(row_out, row_in, row_s, row_r)
    new_coarse_o[...] = new_top
    grad_coarse_o[...] = cot_new + c_back[:, :L]

    second_c = (second - second_mean).astype(BF)
    loads[6].wait()
    finish(grad_out, grad_in, gback_s, gback_r)
    reply = one_hots(send_code.T, CAP, 1)
    cot_mid = (cot_fine[...].astype(F32) + mm(reply, rows_of(grad_in))).astype(BF).astype(F32)
    n_back = layer_back(cot_mid, n_hid, n_norm, n_rstd, n_first[...], n_second[...], n_gain[...])

    def write_grad(i, sl, value):
        grad_v[sl, :] = value
        pltpu.make_async_copy(grad_v.at[sl], grad_edges_o.at[sl], grad_sem.at[i]).start()

    edge_backward(
        snd, rcv, code, s_upper, r_upper, beside(n_back[:, L:].astype(BF)), cot, norm, hid, rstd,
        w_lat, second_c, e_gain[...], s_table, r_table, cot_pre, write_grad,
    )
    back_table = below_each_other(s_table[...]).astype(BF)
    back = mm_nt(back_table[NODES:], w_src)
    ret_out[...] = back.astype(BF).reshape(4, MIRROR, L)
    return_wait = mirrors(
        ret_out, ret_in, ret_s, ret_r, ("below", "above", "left", "right"), ("above", "below", "right", "left")
    )
    total = cot_mid + n_back[:, :L] + mm_nt(back_table[:NODES], w_src)
    total = total + mm_nt(below_each_other(r_table[...]).astype(BF), w_tgt)
    finish(row_out, row_in, row_s, row_r)
    new_nodes_o[...] = (middle.astype(F32) + mm(reply, rows_of(row_in))).astype(BF)
    return_wait()
    grad_nodes_o[...] = total + mm(one_hots(chosen_code, 4, 0), ret_in[...].reshape(4 * MIRROR, L))
    for i in range(STEPS):
        sl = pl.ds(i * CHUNK, CHUNK)
        pltpu.make_async_copy(new_v.at[sl], new_edges_o.at[sl], new_sem.at[i]).wait()
        pltpu.make_async_copy(grad_v.at[sl], grad_edges_o.at[sl], grad_sem.at[i]).wait()


def finish_kernel(*refs):
    ins, outs, held, (wide, load_sems, sems) = refs[:6], refs[6:12], refs[12:18], refs[18:]
    work = []
    for k in (4, 1, 0, 3, 2, 5):
        rows = ins[k].shape[0]
        count = PARTS if rows == EDGES else 1
        for i in range(count):
            sl = pl.ds(i * (rows // count), rows // count)
            n = len(work)
            final = wide if k == 4 else held[k]
            work.append((
                k, sl,
                pltpu.make_async_copy(ins[k].at[sl], held[k].at[sl], load_sems.at[n]),
                pltpu.make_async_copy(final.at[sl], outs[k].at[sl], sems.at[n]),
            ))
    for k, sl, load, store in work:
        load.start()
    for k, sl, load, store in work:
        load.wait()
        if k == 4:
            wide[sl, :] = held[k][sl, :].astype(F32)
        store.start()
    for k, sl, load, store in work:
        store.wait()


VM = pl.BlockSpec(memory_space=pltpu.VMEM)
HBM = pl.BlockSpec(memory_space=pltpu.HBM)
ANY = pl.BlockSpec(memory_space=pl.ANY)


def shaped(*sizes, dtype=BF):
    return jax.ShapeDtypeStruct(sizes, dtype)


def local(
    nodes, edges, coarse, senders, receivers, mirror_rows, owner_device, owner_slot,
    edge_first, edge_bias, edge_second, edge_gain, node_first, node_bias, node_second, node_gain,
    coarse_first, coarse_bias, coarse_second, coarse_gain, cot_nodes, cot_edges, cot_coarse,
):
    def line(v):
        return v.reshape(1, -1)

    edge_rows = [pltpu.VMEM((EDGES, L), BF)] * 9
    pair = lambda *sizes: [pltpu.VMEM(sizes, BF)] * 2
    dma = pltpu.SemaphoreType.DMA
    ins = (
        line(senders), line(receivers), mirror_rows[0, 0], line(owner_device), line(owner_slot),
        edges[0, 0], cot_edges[0, 0], nodes[0, 0], coarse[0, 0], cot_nodes[0, 0], cot_coarse[0, 0],
        edge_first, line(edge_bias), edge_second, line(edge_gain),
        node_first, line(node_bias), node_second, line(node_gain),
        coarse_first, line(coarse_bias), coarse_second, line(coarse_gain),
    )
    outs = pl.pallas_call(
        kernel,
        out_shape=[
            shaped(NODES, L), shaped(EDGES, L), shaped(128, L),
            shaped(NODES, L, dtype=F32), shaped(EDGES, L), shaped(128, L, dtype=F32),
        ],
        in_specs=[HBM] * INPUTS,
        out_specs=[VM, HBM, VM, VM, HBM, VM],
        scratch_shapes=[pltpu.VMEM(v.shape, v.dtype) for v in ins]
        + edge_rows
        + [
            pltpu.VMEM((S_HALF, 2 * L), BF), pltpu.VMEM((R_HALF, 2 * L), BF), pltpu.VMEM((NODES, 2 * L), F32), pltpu.VMEM((S_HALF, 2 * L), F32),
            pltpu.VMEM((R_HALF, 2 * L), F32),
            pltpu.VMEM((DEVICES * CAP, NODES), BF),
        ]
        + pair(4, MIRROR, L) + pair(DEVICES, 2 * CAP, L) + pair(DEVICES, CAP, L) * 3 + pair(4, MIRROR, L)
        + [dma((INPUTS,)), dma((STEPS,)), dma((STEPS,))] + [dma((4,))] * 4 + [dma] * 8,
        compiler_params=pltpu.CompilerParams(
            vmem_limit_bytes=58 << 20, collective_id=0, has_side_effects=True
        ),
        name="mesh_layer",
    )(*ins)
    outs = pl.pallas_call(
        finish_kernel,
        out_shape=[
            shaped(NODES, L), shaped(EDGES, L), shaped(128, L),
            shaped(NODES, L, dtype=F32), shaped(EDGES, L, dtype=F32), shaped(128, L, dtype=F32),
        ],
        in_specs=[HBM] * 6,
        out_specs=[HBM] * 6,
        scratch_shapes=[pltpu.VMEM(v.shape, v.dtype) for v in outs]
        + [pltpu.VMEM((EDGES, L), F32)] + [dma((2 * PARTS + 4,))] * 2,
        compiler_params=pltpu.CompilerParams(vmem_limit_bytes=58 << 20),
        name="write_results",
    )(*outs)
    return tuple(o[None, None] for o in outs)


def solution(mesh):
    four, three, whole = P("dom", "slab", None, None), P("dom", "slab", None), P()
    in_specs = (four, four, four, three, three, four, four, three) + (whole,) * 12 + (four,) * 3
    return jax.shard_map(local, mesh=mesh, in_specs=in_specs, out_specs=(four,) * 6, check_vma=False)
```

```python
import functools

import jax
import jax.numpy as jnp
from jax import lax
from jax.experimental import pallas as pl
from jax.experimental.pallas import tpu as pltpu
from jax.sharding import PartitionSpec as P

eps = 1e-05
BF = jnp.bfloat16
F32 = jnp.float32
MESH = pl.DeviceIdType.MESH
DOM, SLAB, DEVICES = 8, 16, 128
NODES, EDGES, MIRROR, CAP, L = 512, 8192, 64, 8, 128
CHUNK = 2048
STEPS = EDGES // CHUNK
PARTS = 4
INPUTS = 23
FIRST = (7, 2, 3, 4, 9)
LAST = (5, 6)
S_HALF, R_HALF = 384, 256


def mm(a, b):
    return lax.dot_general(a, b, (((1,), (0,)), ((), ())), preferred_element_type=F32)


def mm_nt(a, b):
    return lax.dot_general(a, b, (((1,), (1,)), ((), ())), preferred_element_type=F32)


def averager():
    return jnp.full((L, L), 1.0 / L, BF)


def id_code(row):
    n = row.shape[1]
    low = jnp.broadcast_to((row & 127).astype(F32).astype(BF), (128, n))
    high = jnp.broadcast_to((row >> 7).astype(F32).astype(BF), (128, n))
    place = lax.broadcasted_iota(jnp.int32, (128, n), 0).astype(F32).astype(BF)
    return jnp.where(low == place, high, BF(-1))


def one_hots(code, blocks, axis):
    return jnp.concatenate([jnp.where(code == BF(k), BF(1), BF(0)) for k in range(blocks)], axis)


def halves(x):
    high = x.astype(BF)
    return jnp.concatenate([high, (x - high.astype(F32)).astype(BF)], 1)


def normed(hid, second):
    mixed = mm(hid, second)
    center = mixed - jnp.mean(mixed, 1, keepdims=True)
    rstd = lax.rsqrt(jnp.mean(center * center, 1, keepdims=True) + eps)
    return center * rstd, rstd


def layer(rows, added, first, bias, second):
    pre = mm(jnp.concatenate([rows, added.astype(BF)], 1), first) + bias
    hid = jnp.maximum(pre, 0.0).astype(BF)
    norm, rstd = normed(hid, second)
    return hid, norm, rstd


def layer_back(cot, hid, norm, rstd, first, second, gain):
    scaled = cot * gain
    along = jnp.mean(scaled * norm, 1, keepdims=True)
    cot_mixed = rstd * (scaled - jnp.mean(scaled, 1, keepdims=True) - norm * along)
    cot_hid = mm_nt(cot_mixed.astype(BF), second)
    cot_pre = jnp.where(hid.astype(F32) > 0, cot_hid, 0.0).astype(BF)
    return mm_nt(cot_pre, first)


def staged(first, second, between=None):
    first(0)

    def body(i, carry):
        if between is not None:
            between(i - 1)
        second(i - 1)
        first(i)
        return carry

    lax.fori_loop(1, STEPS, body, 0)
    second(STEPS - 1)


def rows_at(i):
    return pl.ds(i * CHUNK if isinstance(i, int) else pl.multiple_of(i * CHUNK, CHUNK), CHUNK)


def edge_forward(
    snd, rcv, lat, s_side, r_side, first, bias, mixer, gain, norm_o, hid_o, rstd_o, code_o, s_upper, r_upper, sums, write, between
):
    sums[...] = jnp.zeros_like(sums)

    def gather(i):
        sl = rows_at(i)
        for ids, half, upper in ((snd, S_HALF, s_upper), (rcv, R_HALF, r_upper)):
            flag = jnp.where(ids[:, sl] >= half, 1.0, 0.0).astype(BF)
            upper[sl, :] = jnp.broadcast_to(flag, (L, CHUNK)).T
        s_rows, r_rows = id_code(within(snd[:, sl], S_HALF)).T, id_code(within(rcv[:, sl], R_HALF)).T
        code_o[sl, :] = r_rows
        src, tgt = mm(one_hots(s_rows, 3, 1), s_side[...]), mm(one_hots(r_rows, 2, 1), r_side[...])
        src = jnp.where(s_upper[sl, :].astype(F32) > 0, src[:, L:], src[:, :L]).astype(BF)
        tgt = jnp.where(r_upper[sl, :].astype(F32) > 0, tgt[:, L:], tgt[:, :L]).astype(BF)
        pre = mm(jnp.concatenate([lat[sl, :], src, tgt], 1), first) + bias
        hid_o[sl, :] = jnp.maximum(pre, 0.0).astype(BF)

    def update(i):
        sl = rows_at(i)
        mixed = mm(hid_o[sl, :], mixer)
        center = mixed[:, :L] - mixed[:, L:]
        rstd = lax.rsqrt(jnp.mean(center * center, 1, keepdims=True) + eps)
        norm = center * rstd
        norm_o[sl, :] = norm.astype(BF)
        rstd_o[sl, :] = jnp.broadcast_to(rstd, norm.shape).astype(BF)
        change = norm * gain
        write(i, sl, (lat[sl, :].astype(F32) + change).astype(BF))
        sums[...] += mm(one_hots(id_code(rcv[:, sl]), 4, 0), halves(change))

    staged(gather, update, between)


def within(ids, half):
    return jnp.where(ids >= half, ids - half, ids)


def beside(rows):
    half = rows.shape[0] // 2
    return jnp.concatenate([rows[:half], rows[half:]], 1)


def below_each_other(pair):
    return jnp.concatenate([pair[:, :L], pair[:, L:]], 0)


def parted(rows, upper):
    chosen = upper > BF(0)
    return jnp.concatenate([jnp.where(chosen, BF(0), rows), jnp.where(chosen, rows, BF(0))], 1)


def edge_backward(
    snd, rcv, code_i, s_upper, r_upper, cot_table, cot, norm_i, hid_i, rstd_i, second, gain,
    s_table, r_table, pre_o,
):
    s_table[...] = jnp.zeros_like(s_table)
    r_table[...] = jnp.zeros_like(r_table)

    def through(i):
        sl = rows_at(i)
        norm = norm_i[sl, :].astype(F32)
        found = mm(one_hots(code_i[sl, :], 2, 1), cot_table)
        found = jnp.where(r_upper[sl, :].astype(F32) > 0, found[:, L:], found[:, :L])
        scaled = (cot[sl, :].astype(F32) + found) * gain
        along = mm((scaled * norm).astype(BF), averager())
        cot_mixed = (rstd_i[sl, :].astype(F32) * (scaled - norm * along)).astype(BF)
        cot_hid = mm_nt(cot_mixed, second)
        pre_o[sl, :] = jnp.where(hid_i[sl, :].astype(F32) > 0, cot_hid, 0.0).astype(BF)

    def spread(i):
        sl = rows_at(i)
        cot_pre = pre_o[sl, :]
        s_code, r_code = id_code(within(snd[:, sl], S_HALF)), id_code(within(rcv[:, sl], R_HALF))
        s_table[...] += mm(one_hots(s_code, 3, 0), parted(cot_pre, s_upper[sl, :]))
        r_table[...] += mm(one_hots(r_code, 2, 0), parted(cot_pre, r_upper[sl, :]))

    staged(through, spread)


def kernel(*refs):
    sources, targets, rest = refs[:INPUTS], refs[INPUTS + 6 : 2 * INPUTS + 6], refs[2 * INPUTS + 6 :]
    (
        snd, rcv, chosen, own_dev, own_slot, lat, cot, fine, top, cot_fine, cot_top,
        e_first, e_bias, e_second, e_gain, n_first, n_bias, n_second, n_gain, c_first, c_bias, c_second, c_gain,
    ) = targets
    new_nodes_o, new_edges_o, new_coarse_o, grad_nodes_o, grad_edges_o, grad_coarse_o = refs[INPUTS : INPUTS + 6]
    (
        norm, hid, rstd, code, new_v, grad_v, cot_pre, s_upper, r_upper, s_side, r_side, sums, s_table, r_table, pick,
        mir_out, mir_in, early_out, early_in, mid_out, mid_in, grad_out, grad_in, row_out, row_in, ret_out, ret_in,
        load_sem, new_sem, grad_sem, mir_s, mir_r, ret_s, ret_r, early_s, early_r, mid_s, mid_r,
        gback_s, gback_r, row_s, row_r,
    ) = rest
    dom, slab = lax.axis_index("dom"), lax.axis_index("slab")
    me = dom * SLAB + slab

    loads = [pltpu.make_async_copy(src, dst, load_sem.at[k]) for k, (src, dst) in enumerate(zip(sources, targets))]
    for k in FIRST + tuple(k for k in range(INPUTS) if k not in FIRST + LAST) + LAST:
        loads[k].start()

    def peers(act):
        def body(step, carry):
            other = lax.rem(me + step, DEVICES)
            act(other, (other // SLAB, lax.rem(other, SLAB)))
            return carry

        lax.fori_loop(1, DEVICES, body, 0)

    barrier = pltpu.get_barrier_semaphore()
    peers(lambda other, place: pl.semaphore_signal(barrier, inc=1, device_id=place, device_id_type=MESH))

    def exchange(out, land, send, recv):
        def start(other, place):
            pltpu.make_async_remote_copy(
                src_ref=out.at[other], dst_ref=land.at[me], send_sem=send, recv_sem=recv,
                device_id=place, device_id_type=MESH,
            ).start()

        peers(start)
        land[me] = out[me]

    def finish(out, land, send, recv):
        for ref, sem in ((land, recv), (out, send)):
            whole = ref.at[pl.ds(0, DEVICES - 1)]
            pltpu.make_async_copy(whole, whole, sem).wait()

    def blocks(wide):
        return wide.reshape(DEVICES, CAP, L)

    def rows_of(land):
        return land[...].astype(F32).reshape(DEVICES * CAP, L).astype(BF)

    below, above = (dom - 1, slab), (dom + 1, slab)
    left, right = (dom, slab - 1), (dom, slab + 1)
    has = {"below": dom > 0, "above": dom < DOM - 1, "left": slab > 0, "right": slab < SLAB - 1}
    spot = {"below": below, "above": above, "left": left, "right": right}

    def mirrors(out, land, send, recv, targets, sources):
        copies = [
            pltpu.make_async_remote_copy(
                src_ref=out.at[k], dst_ref=land.at[k], send_sem=send.at[k], recv_sem=recv.at[k],
                device_id=spot[targets[k]], device_id_type=MESH,
            )
            for k in range(4)
        ]
        for k in range(4):
            pl.when(has[targets[k]])(copies[k].start)
            pl.when(jnp.logical_not(has[sources[k]]))(lambda k=k: land.__setitem__(k, jnp.zeros((MIRROR, L), BF)))

        def wait():
            for k in range(4):
                pl.when(has[sources[k]])(copies[k].wait_recv)
                pl.when(has[targets[k]])(copies[k].wait_send)

        return wait

    for k, load in enumerate(loads):
        if k not in (5, 6):
            load.wait()

    picked = jnp.concatenate([chosen[k : k + 1, :] for k in range(4)], 1)
    chosen_code = id_code(picked)
    mir_out[...] = mm(one_hots(chosen_code.T, 4, 1), fine[...]).astype(BF).reshape(4, MIRROR, L)

    pl.semaphore_wait(barrier, DEVICES - 1)
    mirror_wait = mirrors(
        mir_out, mir_in, mir_s, mir_r, ("above", "below", "right", "left"), ("below", "above", "left", "right")
    )

    owner = own_dev[...]
    group = one_hots(id_code(owner), 1, 0)
    place = lax.broadcasted_iota(jnp.int32, (NODES, NODES), 0)
    earlier = jnp.where(place < lax.broadcasted_iota(jnp.int32, (NODES, NODES), 1), 1.0, 0.0).astype(BF)
    rank = jnp.sum(mm(group, earlier) * group.astype(F32), 0, keepdims=True)
    send_code = id_code(owner * CAP + rank.astype(jnp.int32))
    pick[...] = one_hots(send_code, CAP, 0)
    slot_rows = jnp.broadcast_to((own_slot[...] + 1).astype(F32).astype(BF), (L, NODES)).T
    early = mm(pick[...], jnp.concatenate([cot_fine[...], slot_rows], 1))
    early_out[...] = jnp.concatenate([blocks(early[:, :L]), blocks(early[:, L:])], 1).astype(BF)
    exchange(early_out, early_in, early_s, early_r)

    w_lat, w_src, w_tgt = e_first[:L, :], e_first[L : 2 * L, :], e_first[2 * L :, :]
    r_side[...] = beside(fine[...])
    second = e_second[...].astype(F32)
    second_mean = jnp.broadcast_to(jnp.mean(second, 1, keepdims=True), (L, L))
    mixer = jnp.concatenate([e_second[...], second_mean.astype(BF)], 1)
    mirror_wait()
    s_side[...] = beside(jnp.concatenate([fine[...], mir_in[...].reshape(4 * MIRROR, L)], 0))
    loads[5].wait()

    def write_new(i, sl, value):
        new_v[sl, :] = value
        pltpu.make_async_copy(new_v.at[sl], new_edges_o.at[sl], new_sem.at[i]).start()

    edge_forward(
        snd, rcv, lat, s_side, r_side, e_first[...], e_bias[...], mixer, e_gain[...], norm, hid, rstd, code, s_upper, r_upper, sums, write_new, None
    )

    summed = sums[:, :L] + sums[:, L:]
    n_hid, n_norm, n_rstd = layer(fine[...], summed, n_first[...], n_bias[...], n_second[...])
    middle = (fine[...].astype(F32) + n_norm * n_gain[...]).astype(BF)
    mid_out[...] = blocks(mm(pick[...], middle)).astype(BF)
    exchange(mid_out, mid_in, mid_s, mid_r)

    finish(early_out, early_in, early_s, early_r)
    early_rows = early_in[...].astype(F32)
    slots = early_rows[:, CAP:].reshape(DEVICES * CAP, L)
    lane = lax.broadcasted_iota(jnp.int32, (DEVICES * CAP, L), 1).astype(F32)
    held = jnp.where(slots == lane + 1.0, 1.0, 0.0).astype(BF)
    gather = held.T
    cot_at = mm(gather, early_rows[:, :CAP].reshape(DEVICES * CAP, L).astype(BF))
    cot_new = (cot_top[...].astype(F32) + cot_at.astype(BF).astype(F32)).astype(BF).astype(F32)
    finish(mid_out, mid_in, mid_s, mid_r)
    pooled = mm(gather, rows_of(mid_in))
    c_hid, c_norm, c_rstd = layer(top[...], pooled, c_first[...], c_bias[...], c_second[...])
    new_top = (top[...].astype(F32) + c_norm * c_gain[...]).astype(BF)
    c_back = layer_back(cot_new, c_hid, c_norm, c_rstd, c_first[...], c_second[...], c_gain[...])
    grad_out[...] = blocks(mm(held, c_back[:, L:].astype(BF))).astype(BF)
    exchange(grad_out, grad_in, gback_s, gback_r)
    row_out[...] = blocks(mm(held, new_top)).astype(BF)
    exchange(row_out, row_in, row_s, row_r)
    new_coarse_o[...] = new_top
    grad_coarse_o[...] = cot_new + c_back[:, :L]

    second_c = (second - second_mean).astype(BF)
    loads[6].wait()
    finish(grad_out, grad_in, gback_s, gback_r)
    reply = one_hots(send_code.T, CAP, 1)
    cot_mid = (cot_fine[...].astype(F32) + mm(reply, rows_of(grad_in))).astype(BF).astype(F32)
    n_back = layer_back(cot_mid, n_hid, n_norm, n_rstd, n_first[...], n_second[...], n_gain[...])

    def write_grad(i, sl, value):
        grad_v[sl, :] = value
        pltpu.make_async_copy(grad_v.at[sl], grad_edges_o.at[sl], grad_sem.at[i]).start()

    edge_backward(
        snd, rcv, code, s_upper, r_upper, beside(n_back[:, L:].astype(BF)), cot, norm, hid, rstd,
        second_c, e_gain[...], s_table, r_table, cot_pre,
    )
    back_table = below_each_other(s_table[...]).astype(BF)
    back = mm_nt(back_table[NODES:], w_src)
    ret_out[...] = back.astype(BF).reshape(4, MIRROR, L)
    return_wait = mirrors(
        ret_out, ret_in, ret_s, ret_r, ("below", "above", "left", "right"), ("above", "below", "right", "left")
    )
    def lat_cotangent(i, carry):
        sl = rows_at(i)
        write_grad(i, sl, (cot[sl, :].astype(F32) + mm_nt(cot_pre[sl, :], w_lat)).astype(BF))
        return carry

    lax.fori_loop(0, STEPS, lat_cotangent, 0)
    total = cot_mid + n_back[:, :L] + mm_nt(back_table[:NODES], w_src)
    total = total + mm_nt(below_each_other(r_table[...]).astype(BF), w_tgt)
    finish(row_out, row_in, row_s, row_r)
    new_nodes_o[...] = (middle.astype(F32) + mm(reply, rows_of(row_in))).astype(BF)
    return_wait()
    grad_nodes_o[...] = total + mm(one_hots(chosen_code, 4, 0), ret_in[...].reshape(4 * MIRROR, L))
    for i in range(STEPS):
        sl = pl.ds(i * CHUNK, CHUNK)
        pltpu.make_async_copy(new_v.at[sl], new_edges_o.at[sl], new_sem.at[i]).wait()
        pltpu.make_async_copy(grad_v.at[sl], grad_edges_o.at[sl], grad_sem.at[i]).wait()


def finish_kernel(*refs):
    ins, outs, held, (wide, load_sems, sems) = refs[:6], refs[6:12], refs[12:18], refs[18:]
    work = []
    for k in (4, 1, 0, 3, 2, 5):
        rows = ins[k].shape[0]
        count = PARTS if rows == EDGES else 1
        for i in range(count):
            sl = pl.ds(i * (rows // count), rows // count)
            n = len(work)
            final = wide if k == 4 else held[k]
            work.append((
                k, sl,
                pltpu.make_async_copy(ins[k].at[sl], held[k].at[sl], load_sems.at[n]),
                pltpu.make_async_copy(final.at[sl], outs[k].at[sl], sems.at[n]),
            ))
    for k, sl, load, store in work:
        load.start()
    for k, sl, load, store in work:
        load.wait()
        if k == 4:
            wide[sl, :] = held[k][sl, :].astype(F32)
        store.start()
    for k, sl, load, store in work:
        store.wait()


VM = pl.BlockSpec(memory_space=pltpu.VMEM)
HBM = pl.BlockSpec(memory_space=pltpu.HBM)
ANY = pl.BlockSpec(memory_space=pl.ANY)


def shaped(*sizes, dtype=BF):
    return jax.ShapeDtypeStruct(sizes, dtype)


def local(
    nodes, edges, coarse, senders, receivers, mirror_rows, owner_device, owner_slot,
    edge_first, edge_bias, edge_second, edge_gain, node_first, node_bias, node_second, node_gain,
    coarse_first, coarse_bias, coarse_second, coarse_gain, cot_nodes, cot_edges, cot_coarse,
):
    def line(v):
        return v.reshape(1, -1)

    edge_rows = [pltpu.VMEM((EDGES, L), BF)] * 9
    pair = lambda *sizes: [pltpu.VMEM(sizes, BF)] * 2
    dma = pltpu.SemaphoreType.DMA
    ins = (
        line(senders), line(receivers), mirror_rows[0, 0], line(owner_device), line(owner_slot),
        edges[0, 0], cot_edges[0, 0], nodes[0, 0], coarse[0, 0], cot_nodes[0, 0], cot_coarse[0, 0],
        edge_first, line(edge_bias), edge_second, line(edge_gain),
        node_first, line(node_bias), node_second, line(node_gain),
        coarse_first, line(coarse_bias), coarse_second, line(coarse_gain),
    )
    outs = pl.pallas_call(
        kernel,
        out_shape=[
            shaped(NODES, L), shaped(EDGES, L), shaped(128, L),
            shaped(NODES, L, dtype=F32), shaped(EDGES, L), shaped(128, L, dtype=F32),
        ],
        in_specs=[HBM] * INPUTS,
        out_specs=[VM, HBM, VM, VM, HBM, VM],
        scratch_shapes=[pltpu.VMEM(v.shape, v.dtype) for v in ins]
        + edge_rows
        + [
            pltpu.VMEM((S_HALF, 2 * L), BF), pltpu.VMEM((R_HALF, 2 * L), BF), pltpu.VMEM((NODES, 2 * L), F32), pltpu.VMEM((S_HALF, 2 * L), F32),
            pltpu.VMEM((R_HALF, 2 * L), F32),
            pltpu.VMEM((DEVICES * CAP, NODES), BF),
        ]
        + pair(4, MIRROR, L) + pair(DEVICES, 2 * CAP, L) + pair(DEVICES, CAP, L) * 3 + pair(4, MIRROR, L)
        + [dma((INPUTS,)), dma((STEPS,)), dma((STEPS,))] + [dma((4,))] * 4 + [dma] * 8,
        compiler_params=pltpu.CompilerParams(
            vmem_limit_bytes=58 << 20, collective_id=0, has_side_effects=True
        ),
        name="mesh_layer",
    )(*ins)
    outs = pl.pallas_call(
        finish_kernel,
        out_shape=[
            shaped(NODES, L), shaped(EDGES, L), shaped(128, L),
            shaped(NODES, L, dtype=F32), shaped(EDGES, L, dtype=F32), shaped(128, L, dtype=F32),
        ],
        in_specs=[HBM] * 6,
        out_specs=[HBM] * 6,
        scratch_shapes=[pltpu.VMEM(v.shape, v.dtype) for v in outs]
        + [pltpu.VMEM((EDGES, L), F32)] + [dma((2 * PARTS + 4,))] * 2,
        compiler_params=pltpu.CompilerParams(vmem_limit_bytes=58 << 20),
        name="write_results",
    )(*outs)
    return tuple(o[None, None] for o in outs)


def solution(mesh):
    four, three, whole = P("dom", "slab", None, None), P("dom", "slab", None), P()
    in_specs = (four, four, four, three, three, four, four, three) + (whole,) * 12 + (four,) * 3
    return jax.shard_map(local, mesh=mesh, in_specs=in_specs, out_specs=(four,) * 6, check_vma=False)
```
